32 devices in a mesh: ctx: 16 (over z, y, x), dp: 2 (over core).
Axes of the slice: x: 2, y: 2, z: 4, core: 2. Of those that a mesh axis runs over, the one named last changes fastest.
Arguments:
- queries: bfloat16 [2, 2048, 2048], P('dp', 'ctx'), may hold values from -110 to 110
- keys: bfloat16 [2, 2048, 512], P('dp', 'ctx'), may hold values from -4 to 4
- values: bfloat16 [2, 2048, 512], P('dp', 'ctx'), may hold values from -4 to 4
- grad_out: bfloat16 [2, 2048, 2048], P('dp', 'ctx'), may hold values from -12 to 12
- sinks: float32 [16], replicated, may hold values from 0 to 6
- doc_ids: int32 [2, 16], P('dp'), may hold values from 0 to 3, never falling along the last dimension, each value on 1 to 8 neighbouring positions
Outputs:
- grad_queries: bfloat16 [2, 2048, 2048], P('dp', 'ctx')
- grad_keys: bfloat16 [2, 2048, 512], P('dp', 'ctx')
- grad_values: bfloat16 [2, 2048, 512], P('dp', 'ctx')
- grad_sinks: float32 [16], replicated
The draws below stay inside these ranges and needn't reach their ends.
All inputs are finite; a program needn't handle non-finite values.
Results may differ from the reference program's by a relative error of at most 0.017.
Values may be sent and summed in bfloat16 or wider, within the bound.
No kernel may reach another device: no remote copies, remote signals or barrier semaphores. Data moves between devices by JAX's collectives and lax.ppermute only.
A program may use at most 64 MiB of HBM per device.

```python
import math
import jax
import jax.numpy as jnp
import numpy as np
from jax import lax

H = 16
KVH = 4
HD = 128
BLOCK = 128
WINDOW = 512
SEQLEN = 2048
SEQS = 2
NBLK = 16


def draw_pair(key):
    key_query = jax.random.fold_in(key, 11)
    key_key = jax.random.fold_in(key, 12)
    keys_raw = jnp.clip(jax.random.normal(key_key, (SEQS, SEQLEN, KVH, HD), jnp.float32), -4.0, 4.0)
    query_raw = jnp.clip(jax.random.normal(key_query, (SEQS, SEQLEN, H, HD), jnp.float32), -4.0, 4.0)
    return (query_raw.reshape(SEQS, SEQLEN, H * HD), keys_raw.reshape(SEQS, SEQLEN, KVH * HD))


def draw_queries(key, part):
    return draw_pair(key)[0].astype(jnp.bfloat16)


def draw_keys(key, part):
    return draw_pair(key)[1].astype(jnp.bfloat16)


def draw_grad_out(key, part):
    positions = jnp.arange(SEQLEN, dtype=jnp.float32) / (SEQLEN - 1)
    sequence_rank = jnp.arange(SEQS, dtype=jnp.float32) / max(SEQS - 1, 1)
    ramp = (1.0 + 2.0 * positions)[None, :, None] * (1.0 + 2.0 * sequence_rank)[:, None, None] / 3.0
    base = jnp.clip(jax.random.normal(key, (SEQS, SEQLEN, H * HD), jnp.float32), -4.0, 4.0)
    return (base * ramp).astype(jnp.bfloat16)


def block_scale(key, shape, shards, smallest, high):
    def one(position, shards_of):
        steps = jax.random.uniform(jax.random.fold_in(jax.random.fold_in(key, 6), position), (shards_of,), jnp.float32, smallest / len(shards), high / len(shards))
        return jnp.repeat(jnp.exp(steps), shape[position] // shards_of).reshape((-1,) + (1,) * (len(shape) - position - 1))

    factor_of = one(*shards[0])
    for cut in shards[1:]:
        factor_of = factor_of * one(*cut)
    return factor_of


def profile(amount, total, limit, skew):
    portions = [(1 << 20) // math.isqrt(standing ** skew) + 1 for standing in range(2, amount + 1)]
    rest, counts = total - limit - (amount - 1), [1] * (amount - 1)
    while rest > 0:
        candidates = [i for i in range(amount - 1) if counts[i] < limit]
        mass, remaining = sum([portions[i] for i in candidates]), rest
        for i in candidates:
            addition = min(limit - counts[i], max(1, remaining * portions[i] // mass), rest)
            counts[i] = counts[i] + addition
            rest = rest - addition
    return np.array([limit] + counts)


def ragged_sizes(key, count, total, most, lean):
    if count == 2:
        one = jax.random.randint(key, (), max(1, total - most), min(most, total - 1) + 1)
        return jnp.stack([one, total - one])
    sizes = jnp.asarray(profile(count, total, most, lean), jnp.int32)
    pairs = (count - 1) // 2
    source_of, receiver = sizes[1:1 + 2 * pairs:2], sizes[2:2 + 2 * pairs:2]
    room = jnp.minimum(source_of - 1, most - receiver)
    passed = jax.random.randint(jax.random.fold_in(key, 1), (pairs,), 0, 1 << 20) % (room + 1)
    sizes = sizes.at[1:1 + 2 * pairs:2].set(source_of - passed).at[2:2 + 2 * pairs:2].set(receiver + passed)
    return sizes[jax.random.permutation(jax.random.fold_in(key, 2), count)]


def scatter_about(stream_key, dims, scale, bound, split=(), kind=jnp.bfloat16):
    result = scale * jax.random.normal(stream_key, dims, jnp.float32)
    if split:
        result = result * block_scale(stream_key, dims, split, -0.22, 0.18)
    return jnp.clip(result, -bound, bound).astype(kind)


def setup_inputs(seed: int = 0) -> dict:
    arg_keys = jax.random.split(jax.random.key(seed), 7)
    return {
        "queries": draw_queries(jax.random.fold_in(arg_keys[6], 71), 0),
        "keys": draw_keys(jax.random.fold_in(arg_keys[6], 71), 0),
        "values": scatter_about(arg_keys[2], (SEQS, SEQLEN, KVH * HD), 1.0, 4.0, ((0, 2), (1, 16))),
        "grad_out": draw_grad_out(jax.random.fold_in(arg_keys[6], 71), 0),
        "sinks": jnp.clip(jax.random.uniform(arg_keys[4], (H,), jnp.float32, 0.0, 6.0), 0.0, 6.0),
        "doc_ids": jax.vmap(lambda own: jnp.searchsorted(jnp.cumsum(ragged_sizes(own, NBLK // 4, NBLK, NBLK // 2, 2)), jnp.arange(NBLK), side="right"))(jax.random.split(arg_keys[5], SEQS)).reshape((SEQS, NBLK)).astype(jnp.int32),
    }


def one_sequence(queries, keys, values, grad_out, doc_row, sinks):
    length = queries.shape[0]
    group_size = H // KVH
    score_scale = HD ** -0.5
    key_count = WINDOW + BLOCK
    pad_keys = jnp.concatenate([jnp.zeros((WINDOW, KVH * HD), jnp.bfloat16), keys], axis=0)
    pad_values = jnp.concatenate([jnp.zeros((WINDOW, KVH * HD), jnp.bfloat16), values], axis=0)
    doc_pos = jnp.concatenate([jnp.full((WINDOW,), -1, jnp.int32), jnp.repeat(doc_row, BLOCK).astype(jnp.int32)])
    sink_grid = sinks.reshape(KVH, group_size)[:, :, None]

    def block_step(carried, start_row):
        key_grad, value_grad, sink_grad = carried
        q_block = lax.dynamic_slice_in_dim(queries, start_row, BLOCK, 0).reshape(BLOCK, KVH, group_size, HD).astype(jnp.float32)
        g_block = lax.dynamic_slice_in_dim(grad_out, start_row, BLOCK, 0).reshape(BLOCK, KVH, group_size, HD).astype(jnp.float32)
        k_block = lax.dynamic_slice_in_dim(pad_keys, start_row, key_count, 0).reshape(key_count, KVH, HD).astype(jnp.float32)
        v_block = lax.dynamic_slice_in_dim(pad_values, start_row, key_count, 0).reshape(key_count, KVH, HD).astype(jnp.float32)
        query_docs = lax.dynamic_slice_in_dim(doc_pos, start_row + WINDOW, BLOCK, 0)
        key_docs = lax.dynamic_slice_in_dim(doc_pos, start_row, key_count, 0)
        offsets = WINDOW + jnp.arange(BLOCK, dtype=jnp.int32)[:, None] - jnp.arange(key_count, dtype=jnp.int32)[None, :]
        allowed = (query_docs[:, None] == key_docs[None, :]) & (offsets >= 0) & (offsets < WINDOW)
        scores = jnp.einsum('tghd,kgd->ghtk', q_block, k_block) * score_scale
        masked = jnp.where(allowed[None, None], scores, -jnp.inf)
        top_score = jnp.maximum(jnp.max(masked, axis=-1), sink_grid)
        raised = jnp.exp(masked - top_score[..., None])
        sink_weight = jnp.exp(sink_grid - top_score)
        summed = sink_weight + jnp.sum(raised, axis=-1)
        probs = lax.optimization_barrier((raised / summed[..., None]).astype(jnp.bfloat16)).astype(jnp.float32)
        attended = jnp.einsum('ghtk,kgd->tghd', probs, v_block)
        delta = jnp.transpose(jnp.sum(g_block * attended, axis=-1), (1, 2, 0))
        sink_grad = sink_grad - jnp.sum(sink_weight / summed * delta, axis=-1).reshape(H)
        grad_probs = jnp.einsum('tghd,kgd->ghtk', g_block, v_block)
        grad_scores = lax.optimization_barrier((probs * (grad_probs - delta[..., None])).astype(jnp.bfloat16)).astype(jnp.float32)
        query_grad = (jnp.einsum('ghtk,kgd->tghd', grad_scores, k_block) * score_scale).astype(jnp.bfloat16).reshape(BLOCK, H * HD)
        key_part = jnp.einsum('ghtk,tghd->kgd', grad_scores, q_block) * score_scale
        value_part = jnp.einsum('ghtk,tghd->kgd', probs, g_block)
        key_grad = lax.dynamic_update_slice_in_dim(key_grad, lax.dynamic_slice_in_dim(key_grad, start_row, key_count, 0) + key_part.reshape(key_count, KVH * HD), start_row, 0)
        value_grad = lax.dynamic_update_slice_in_dim(value_grad, lax.dynamic_slice_in_dim(value_grad, start_row, key_count, 0) + value_part.reshape(key_count, KVH * HD), start_row, 0)
        return (key_grad, value_grad, sink_grad), query_grad

    starts = jnp.arange(0, length, BLOCK, dtype=jnp.int32)
    initial = (jnp.zeros((length + WINDOW, KVH * HD), jnp.float32), jnp.zeros((length + WINDOW, KVH * HD), jnp.float32), jnp.zeros((H,), jnp.float32))
    final, query_blocks = lax.scan(block_step, initial, starts)
    key_grad, value_grad, sink_grad = final
    return query_blocks.reshape(length, H * HD), key_grad[WINDOW:].astype(jnp.bfloat16), value_grad[WINDOW:].astype(jnp.bfloat16), sink_grad


def reference(queries, keys, values, grad_out, sinks, doc_ids):
    def per_sequence(items):
        return one_sequence(items[0], items[1], items[2], items[3], items[4], sinks)

    grad_q, grad_k, grad_v, sink_parts = lax.map(per_sequence, (queries, keys, values, grad_out, doc_ids))
    return grad_q, grad_k, grad_v, jnp.sum(sink_parts, axis=0)
```

```python
import functools

import jax
import jax.numpy as jnp
from jax import lax
from jax.experimental import pallas as pl
from jax.experimental.pallas import tpu as pltpu
from jax.sharding import PartitionSpec as P

WINDOW = 512
LOG2E = 1.4426950408889634
PARTS = 1

F32 = jnp.float32
BF16 = jnp.bfloat16


def dot_nt(a, b):
    return lax.dot_general(a, b, (((1,), (1,)), ((), ())), preferred_element_type=F32)


def dot_nn(a, b):
    return lax.dot_general(a, b, (((1,), (0,)), ((), ())), preferred_element_type=F32)


def dot_tn(a, b):
    return lax.dot_general(a, b, (((0,), (0,)), ((), ())), preferred_element_type=F32)


def attention_kernel(
    part, kv_heads, group, reach, rows, size,
    place_ref, docs_ref, sinks_ref, q_ref, g_ref, k_ref, v_ref, *refs,
):
    received, outs = refs[:reach], refs[reach:]
    if part:
        outs = outs[1:]
    dq_ref, dsink_ref, own_ref, zown_ref = outs[:4]
    message_refs = outs[4:]
    place = place_ref[0]
    slot = lax.rem(place, reach)
    doc = docs_ref[0, place]

    def same_doc(distance):
        other = docs_ref[0, jnp.maximum(place - distance, 0)]
        return jnp.logical_and(place >= distance, other == doc)

    in_plane = []
    for step in range(1, reach):
        partner = lax.bitwise_xor(slot, step)
        in_plane.append(same_doc(lax.rem(slot - partner + reach, reach)))
    z_cap = jnp.where(same_doc(reach), jnp.inf, -jnp.inf)
    scale = size ** (-0.5)
    to_log2 = scale * LOG2E
    columns = group * rows
    key_at = lax.broadcasted_iota(jnp.int32, (rows, columns), 0)
    query_at = lax.rem(lax.broadcasted_iota(jnp.int32, (rows, columns), 1), rows)
    causal = key_at <= query_at
    lane = lax.broadcasted_iota(jnp.int32, (1, 128), 1)
    sink_row = jnp.zeros((1, 128), F32)
    width = kv_heads * size

    for head in range(kv_heads):
        cut = slice(head * size, (head + 1) * size)
        cut_v = slice(width + head * size, width + (head + 1) * size)
        members = [slice((head * group + j) * size, (head * group + j + 1) * size) for j in range(group)]
        q = jnp.concatenate([q_ref[:, m] for m in members], axis=0)
        g = jnp.concatenate([g_ref[:, m] for m in members], axis=0)
        keys = jnp.concatenate([k_ref[:, cut]] + [r[:, cut] for r in received], axis=0)
        values = jnp.concatenate([v_ref[:, cut]] + [r[:, cut_v] for r in received], axis=0)
        scores = dot_nt(keys, q)
        gprobs = dot_nt(values, g)

        def block(x, i):
            return x[i * rows:(i + 1) * rows]

        s_blocks = [jnp.where(causal, block(scores, 0), jnp.minimum(block(scores, reach), z_cap))]
        t_blocks = [jnp.where(causal, block(gprobs, 0), block(gprobs, reach))]
        for i in range(1, reach):
            s_blocks.append(block(scores, i))
            t_blocks.append(block(gprobs, i))
        flags = [None] + in_plane
        top = jnp.concatenate(
            [jnp.full((1, rows), sinks_ref[(part * kv_heads + head) * group + j] * LOG2E, F32) for j in range(group)],
            axis=1,
        )
        sink_log = top
        for s, flag in zip(s_blocks, flags):
            high = jnp.max(s, axis=0, keepdims=True) * to_log2
            top = jnp.maximum(top, high if flag is None else jnp.where(flag, high, -jnp.inf))
        sink_weight = jnp.exp2(sink_log - top)
        summed = sink_weight
        raised = []
        for s, flag in zip(s_blocks, flags):
            e = jnp.exp2(s * to_log2 - (top if flag is None else jnp.where(flag, top, jnp.inf)))
            summed = summed + jnp.sum(e, axis=0, keepdims=True)
            raised.append(e)
        inverse = 1.0 / summed
        probs = [(e * inverse).astype(BF16) for e in raised]
        delta = jnp.zeros((1, columns), F32)
        for p, t in zip(probs, t_blocks):
            delta = delta + jnp.sum(p.astype(F32) * t, axis=0, keepdims=True)
        gscores = [(p.astype(F32) * (t - delta)).astype(BF16) for p, t in zip(probs, t_blocks)]
        zero = jnp.zeros((), BF16)
        p_all = jnp.concatenate(
            [jnp.where(causal, probs[0], zero)] + probs[1:] + [jnp.where(causal, zero, probs[0])], axis=0
        )
        d_all = jnp.concatenate(
            [jnp.where(causal, gscores[0], zero)] + gscores[1:] + [jnp.where(causal, zero, gscores[0])], axis=0
        )
        dv = dot_nn(p_all, g)
        dk = dot_nn(d_all, q) * scale
        dq = (dot_tn(d_all, keys) * scale).astype(BF16)
        for j, m in enumerate(members):
            dq_ref[:, m] = dq[j * rows:(j + 1) * rows]
        own_ref[:, cut] = block(dk, 0)
        own_ref[:, cut_v] = block(dv, 0)
        zown_ref[:, cut] = block(dk, reach)
        zown_ref[:, cut_v] = block(dv, reach)
        for i, ref in enumerate(message_refs):
            ref[:, cut] = block(dk, i + 1).astype(BF16)
            ref[:, cut_v] = block(dv, i + 1).astype(BF16)
        sink_terms = sink_weight * inverse * delta
        for j in range(group):
            term = jnp.sum(sink_terms[:, j * rows:(j + 1) * rows], axis=1, keepdims=True)
            at = (part * kv_heads + head) * group + j
            sink_row = jnp.where(lane == at, -term, sink_row)
    dsink_ref[...] = sink_row


def attention(part, reach, place, docs, sinks, queries, grad_out, keys, values, received, earlier):
    rows, q_width = queries.shape
    size = q_width // sinks.shape[0]
    kv_width = keys.shape[1] // PARTS
    kv_heads = kv_width // size
    group = sinks.shape[0] * size // keys.shape[1]
    smem = pl.BlockSpec(memory_space=pltpu.SMEM)

    def columns(width, at):
        return pl.BlockSpec((rows, width), lambda i: (0, at))

    q_spec = columns(q_width // PARTS, part)
    kv_spec = columns(kv_width, part)
    pair_spec = columns(2 * kv_width, 0)
    in_specs = [smem] * 3 + [q_spec] * 2 + [kv_spec] * 2 + [pair_spec] * reach
    operands = [place, docs, sinks, queries, grad_out, keys, values, *received]
    aliases = {}
    if part:
        aliases = {len(operands): 0}
        in_specs.append(pl.BlockSpec(memory_space=pl.ANY))
        operands.append(earlier)
    wide = jax.ShapeDtypeStruct((rows, 2 * kv_width), F32)
    narrow = jax.ShapeDtypeStruct((rows, 2 * kv_width), BF16)
    return pl.pallas_call(
        functools.partial(attention_kernel, part, kv_heads, group, reach, rows, size),
        grid=(1,),
        out_shape=[
            jax.ShapeDtypeStruct(queries.shape, BF16), jax.ShapeDtypeStruct((1, 128), F32), wide, wide,
        ] + [narrow] * (reach - 1),
        in_specs=in_specs,
        out_specs=[q_spec, pl.BlockSpec((1, 128), lambda i: (0, 0)), pair_spec, pair_spec]
        + [pair_spec] * (reach - 1),
        input_output_aliases=aliases,
        compiler_params=pltpu.CompilerParams(vmem_limit_bytes=48 * 1024 * 1024),
        cost_estimate=pl.CostEstimate(
            flops=10 * rows * group * rows * (reach + 1) * size * kv_heads,
            bytes_accessed=6 * rows * q_width // PARTS + 20 * rows * reach * kv_width,
            transcendentals=rows * group * rows * reach * kv_heads,
        ),
    )(*operands)


def local(queries, keys, values, grad_out, sinks, doc_ids):
    rows = queries.shape[1]
    reach = WINDOW // rows
    count = lax.axis_size("ctx")
    place = lax.axis_index("ctx")
    slot = lax.rem(place, reach)
    queries, keys, values, grad_out = queries[0], keys[0], values[0], grad_out[0]
    kv_width = keys.shape[1] // PARTS

    def along(x, distance):
        first, last = max(0, -distance), min(count, count - distance)
        return lax.ppermute(x, "ctx", [(i, i + distance) for i in range(first, last)])

    def exchanged(x, step, axis="ctx"):
        return lax.ppermute(x, axis, [(i, i ^ step) for i in range(lax.axis_size(axis))])

    own = [
        jnp.concatenate([x[:, p * kv_width:(p + 1) * kv_width] for x in (keys, values)], axis=1) for p in range(PARTS)
    ]
    received = []
    for p in range(PARTS):
        before = along(own[p], reach)
        arrived = []
        for step in range(1, reach):
            send_own = lax.bitwise_xor(slot, step) > slot
            arrived.append(exchanged(jnp.where(send_own, own[p], before), step))
        received.append(arrived + [before])
    place_row = jnp.full((1,), place, jnp.int32)
    grad_queries = None
    sink_row = jnp.zeros((1, 128), F32)
    shares = []
    for p in range(PARTS):
        grad_queries, sink_part, *share = attention(
            p, reach, place_row, doc_ids, sinks, queries, grad_out, keys, values, received[p], grad_queries
        )
        sink_row = sink_row + sink_part
        shares.append(share)
    totals = []
    for own_sum, before_sum, *messages in shares:
        for step, message in enumerate(messages, 1):
            back = exchanged(message, step).astype(F32)
            mine = lax.bitwise_xor(slot, step) > slot
            own_sum = own_sum + jnp.where(mine, back, 0.0)
            before_sum = before_sum + jnp.where(mine, 0.0, back)
        totals.append((own_sum, along(before_sum.astype(BF16), -reach)))
    sink_row = sink_row + exchanged(sink_row, 1, "dp") if lax.axis_size("dp") == 2 else lax.psum(sink_row, "dp")
    step = 1
    while step < count:
        sink_row = sink_row + exchanged(sink_row, step)
        step *= 2
    whole = [own_sum + last.astype(F32) for own_sum, last in totals]
    grad_keys = jnp.concatenate([w[:, :kv_width] for w in whole], axis=1).astype(BF16)
    grad_values = jnp.concatenate([w[:, kv_width:] for w in whole], axis=1).astype(BF16)
    return grad_queries[None], grad_keys[None], grad_values[None], sink_row[0, : sinks.shape[0]]


def solution(mesh):
    blocks = P("dp", "ctx", None)
    in_specs = (blocks, blocks, blocks, blocks, P(), P("dp", None))
    out_specs = (blocks, blocks, blocks, P())
    return jax.shard_map(local, mesh=mesh, in_specs=in_specs, out_specs=out_specs, check_vma=False)
```

```python
import functools

import jax
import jax.numpy as jnp
from jax import lax
from jax.experimental import pallas as pl
from jax.experimental.pallas import tpu as pltpu
from jax.sharding import PartitionSpec as P

WINDOW = 512
LOG2E = 1.4426950408889634
PARTS = 2

F32 = jnp.float32
BF16 = jnp.bfloat16
SMEM = pl.BlockSpec(memory_space=pltpu.SMEM)
VMEM = pl.BlockSpec(memory_space=pltpu.VMEM)


def dot_nt(a, b):
    return lax.dot_general(a, b, (((1,), (1,)), ((), ())), preferred_element_type=F32)


def dot_nn(a, b):
    return lax.dot_general(a, b, (((1,), (0,)), ((), ())), preferred_element_type=F32)


def dot_tn(a, b):
    return lax.dot_general(a, b, (((0,), (0,)), ((), ())), preferred_element_type=F32)


def kernel_call(body, out_shape, in_specs, operands, flops=0, bytes_accessed=0, transcendentals=0, **options):
    return pl.pallas_call(
        body,
        out_shape=out_shape,
        in_specs=in_specs,
        compiler_params=pltpu.CompilerParams(vmem_limit_bytes=24 * 1024 * 1024),
        cost_estimate=pl.CostEstimate(
            flops=flops, bytes_accessed=bytes_accessed, transcendentals=transcendentals
        ),
        **options,
    )(*operands)


def later(slot, step):
    return lax.bitwise_xor(slot, step) > slot


def prepare_kernel(reach, rows, group, place_ref, docs_ref, sinks_ref, k_ref, v_ref, caps_ref, tops_ref, *own_refs):
    place = place_ref[0]
    slot = lax.rem(place, reach)
    doc = docs_ref[0, place]
    width = k_ref.shape[1] // len(own_refs)
    for part, ref in enumerate(own_refs):
        ref[:, :width] = k_ref[:, part * width:(part + 1) * width]
        ref[:, width:] = v_ref[:, part * width:(part + 1) * width]
    columns = caps_ref.shape[1]
    for step in range(1, reach + 1):
        distance = reach
        if step < reach:
            distance = lax.rem(slot - lax.bitwise_xor(slot, step) + reach, reach)
        other = docs_ref[0, jnp.maximum(place - distance, 0)]
        same = jnp.logical_and(place >= distance, other == doc)
        caps_ref[step:step + 1, :] = jnp.full((1, columns), jnp.where(same, jnp.inf, -jnp.inf), F32)
    for head in range(sinks_ref.shape[0] // group):
        for j in range(group):
            tops_ref[head:head + 1, j * rows:(j + 1) * rows] = jnp.full(
                (1, rows), sinks_ref[head * group + j] * LOG2E, F32
            )


def choose_kernel(reach, place_ref, own_ref, before_ref, *out_refs):
    slot = lax.rem(place_ref[0], reach)
    for bit, ref in enumerate(out_refs):
        @pl.when(later(slot, 1 << bit))
        def _():
            ref[...] = own_ref[...]

        @pl.when(jnp.logical_not(later(slot, 1 << bit)))
        def _():
            ref[...] = before_ref[...]


def attention_kernel(part, kv_heads, group, reach, rows, size, caps_ref, tops_ref, q_ref, g_ref, *refs):
    blocks, outs = refs[:reach + 1], refs[reach + 1:]
    if part:
        sink_before, outs = outs[0], outs[1:]
    sink_ref, own_ref, before_ref, gscores_ref = outs[:4]
    message_refs = outs[4:]
    scale = size ** (-0.5)
    to_log2 = scale * LOG2E
    columns = group * rows
    key_at = lax.broadcasted_iota(jnp.int32, (rows, columns), 0)
    query_at = lax.rem(lax.broadcasted_iota(jnp.int32, (rows, columns), 1), rows)
    causal = key_at <= query_at
    lane = lax.broadcasted_iota(jnp.int32, (1, 128), 1)
    sink_row = sink_before[...] if part else jnp.zeros((1, 128), F32)
    width = kv_heads * size
    zero = jnp.zeros((), BF16)

    def block(x, i):
        return x[i * rows:(i + 1) * rows]

    caps = [caps_ref[i:i + 1, :] for i in range(reach + 1)]
    for head in range(kv_heads):
        cut = slice(head * size, (head + 1) * size)
        cut_v = slice(width + head * size, width + (head + 1) * size)
        first = (part * kv_heads + head) * group
        members = [slice((first + j) * size, (first + j + 1) * size) for j in range(group)]
        q = jnp.concatenate([q_ref[:, m] for m in members], axis=0)
        g = jnp.concatenate([g_ref[:, m] for m in members], axis=0)
        keys = jnp.concatenate([r[:, cut] for r in blocks], axis=0)
        values = jnp.concatenate([r[:, cut_v] for r in blocks], axis=0)
        scores = dot_nt(keys, q)
        gprobs = dot_nt(values, g)
        s_blocks = [jnp.where(causal, block(scores, 0), jnp.minimum(block(scores, reach), caps[reach]))]
        t_blocks = [jnp.where(causal, block(gprobs, 0), block(gprobs, reach))]
        for i in range(1, reach):
            s_blocks.append(block(scores, i))
            t_blocks.append(block(gprobs, i))
        top = tops_ref[part * kv_heads + head:part * kv_heads + head + 1, :]
        sink_log = top
        for i, s in enumerate(s_blocks):
            high = jnp.max(s, axis=0, keepdims=True) * to_log2
            top = jnp.maximum(top, jnp.minimum(high, caps[i]) if i else high)
        sink_weight = jnp.exp2(sink_log - top)
        summed = sink_weight
        raised = []
        for i, s in enumerate(s_blocks):
            e = jnp.exp2(s * to_log2 - (jnp.maximum(top, -caps[i]) if i else top))
            summed = summed + jnp.sum(e, axis=0, keepdims=True)
            raised.append(e)
        inverse = 1.0 / summed
        probs = [(e * inverse).astype(BF16) for e in raised]
        delta = jnp.zeros((1, columns), F32)
        for p, t in zip(probs, t_blocks):
            delta = delta + jnp.sum(p.astype(F32) * t, axis=0, keepdims=True)
        gscores = [(p.astype(F32) * (t - delta)).astype(BF16) for p, t in zip(probs, t_blocks)]
        p_all = jnp.concatenate(
            [jnp.where(causal, probs[0], zero)] + probs[1:] + [jnp.where(causal, zero, probs[0])], axis=0
        )
        d_all = jnp.concatenate(
            [jnp.where(causal, gscores[0], zero)] + gscores[1:] + [jnp.where(causal, zero, gscores[0])], axis=0
        )
        dv = dot_nn(p_all, g)
        dk = dot_nn(d_all, q) * scale
        gscores_ref[head * (reach + 1) * rows:(head + 1) * (reach + 1) * rows, :] = d_all
        own_ref[:, cut] = block(dk, 0)
        own_ref[:, cut_v] = block(dv, 0)
        before_ref[:, cut] = block(dk, reach)
        before_ref[:, cut_v] = block(dv, reach)
        for i, ref in enumerate(message_refs):
            ref[:, cut] = block(dk, i + 1).astype(BF16)
            ref[:, cut_v] = block(dv, i + 1).astype(BF16)
        sink_terms = sink_weight * inverse * delta
        for j in range(group):
            term = jnp.sum(sink_terms[:, j * rows:(j + 1) * rows], axis=1, keepdims=True)
            sink_row = jnp.where(lane == first + j, -term, sink_row)
    sink_ref[...] = sink_row


def queries_kernel(kv_heads, group, reach, rows, size, *refs):
    parts = len(refs) // (reach + 2)
    *ins, dq_ref, done_ref = refs
    scale = size ** (-0.5)
    span = (reach + 1) * rows
    for part in range(parts):
        gscores_ref, *blocks = ins[part * (reach + 2):(part + 1) * (reach + 2)]
        for head in range(kv_heads):
            cut = slice(head * size, (head + 1) * size)
            keys = jnp.concatenate([r[:, cut] for r in blocks], axis=0)
            dq = (dot_tn(gscores_ref[head * span:(head + 1) * span, :], keys) * scale).astype(BF16)
            for j in range(group):
                at = ((part * kv_heads + head) * group + j) * size
                dq_ref[:, at:at + size] = dq[j * rows:(j + 1) * rows]
    done_ref[...] = jnp.zeros_like(done_ref)


def combine_kernel(reach, place_ref, pass_ref, own_ref, before_ref, *refs):
    *messages, own_out, before_out, pass_out = refs
    slot = lax.rem(place_ref[0], reach)
    own, before = own_ref[...], before_ref[...]
    for step, message in enumerate(messages, 1):
        mine = later(slot, step)
        back = message[...].astype(F32)
        own = own + jnp.where(mine, back, 0.0)
        before = before + jnp.where(mine, 0.0, back)
    own_out[...] = own
    before_out[...] = before.astype(BF16)
    pass_out[...] = pass_ref[...]


def finish_kernel(parts, sink_ref, *refs):
    owns, lasts = refs[:parts], refs[parts:2 * parts]
    dk_ref, dv_ref, dsink_ref = refs[2 * parts:]
    width = dk_ref.shape[1] // parts
    for part in range(parts):
        total = owns[part][...] + lasts[part][...].astype(F32)
        cut = slice(part * width, (part + 1) * width)
        dk_ref[:, cut] = total[:, :width].astype(BF16)
        dv_ref[:, cut] = total[:, width:].astype(BF16)
    dsink_ref[...] = sink_ref[0, :dsink_ref.shape[0]]


def local(queries, keys, values, grad_out, sinks, doc_ids):
    rows, q_width = queries.shape[1:]
    kv_width = keys.shape[2]
    heads = sinks.shape[0]
    size = q_width // heads
    group = q_width // kv_width
    kv_heads = kv_width // size // PARTS
    reach = WINDOW // rows
    count = lax.axis_size("ctx")
    place = jnp.full((1,), lax.axis_index("ctx"), jnp.int32)
    queries, keys, values, grad_out = queries[0], keys[0], values[0], grad_out[0]
    wide = jax.ShapeDtypeStruct((rows, 2 * kv_width // PARTS), F32)
    narrow = jax.ShapeDtypeStruct(wide.shape, BF16)
    row = jax.ShapeDtypeStruct((1, 128), F32)
    table = jax.ShapeDtypeStruct((8 * (-(-max(reach + 1, heads // group) // 8)), group * rows), F32)
    span = (reach + 1) * rows

    def along(x, distance):
        first, last = max(0, -distance), min(count, count - distance)
        return lax.ppermute(x, "ctx", [(i, i + distance) for i in range(first, last)])

    def exchanged(x, step, axis="ctx"):
        return lax.ppermute(x, axis, [(i, i ^ step) for i in range(lax.axis_size(axis))])

    caps, tops, *own = kernel_call(
        functools.partial(prepare_kernel, reach, rows, group),
        [table, table] + [narrow] * PARTS,
        [SMEM] * 3 + [VMEM] * 2,
        (place, doc_ids, sinks, keys, values),
        bytes_accessed=8 * rows * kv_width,
    )
    bits = reach.bit_length() - 1
    before = [along(x, reach) for x in own]
    blocks = []
    for p in range(PARTS):
        chosen = kernel_call(
            functools.partial(choose_kernel, reach),
            [narrow] * bits,
            [SMEM] + [VMEM] * 2,
            (place, own[p], before[p]),
            bytes_accessed=bits * 8 * rows * kv_width // PARTS,
        )
        arrived = [exchanged(chosen[step.bit_length() - 1], step) for step in range(1, reach)]
        blocks.append([own[p], *arrived, before[p]])
    sink_row = None
    shares, gscores = [], []
    for p in range(PARTS):
        sink_row, own_sum, before_sum, part_gscores, *messages = kernel_call(
            functools.partial(attention_kernel, p, kv_heads, group, reach, rows, size),
            [row, wide, wide, jax.ShapeDtypeStruct((kv_heads * span, group * rows), BF16)] + [narrow] * (reach - 1),
            [VMEM] * (5 + reach + (p > 0)),
            (caps, tops, queries, grad_out, *blocks[p]) + ((sink_row,) if p else ()),
            flops=8 * rows * group * span * size * kv_heads,
            bytes_accessed=8 * rows * q_width // PARTS + 20 * span * kv_width // PARTS,
            transcendentals=group * rows * span * kv_heads,
        )
        gscores.append(part_gscores)
        shares.append((own_sum, before_sum, [exchanged(m, step) for step, m in enumerate(messages, 1)]))
    grad_queries, done = kernel_call(
        functools.partial(queries_kernel, kv_heads, group, reach, rows, size),
        [jax.ShapeDtypeStruct(queries.shape, BF16), row],
        [VMEM] * (PARTS * (reach + 2)),
        [x for p in range(PARTS) for x in (gscores[p], *blocks[p])],
        flops=2 * rows * group * span * size * kv_heads * PARTS,
        bytes_accessed=2 * rows * q_width + 2 * group * rows * span * kv_heads * PARTS,
    )
    if lax.axis_size("dp") == 2:
        sink_row = sink_row + exchanged(sink_row, 1, "dp")
    else:
        sink_row = lax.psum(sink_row, "dp")
    step = reach
    while step < count:
        sink_row = sink_row + exchanged(sink_row, step)
        step *= 2
    passing = [done] * (PARTS - 1) + [sink_row + done]
    owns, lasts = [], []
    for p in range(PARTS):
        own_sum, before_sum, back = shares[p]
        own_sum, before_sum, sink_row = kernel_call(
            functools.partial(combine_kernel, reach),
            [wide, narrow, row],
            [SMEM] + [VMEM] * (reach + 2),
            (place, passing[p], own_sum, before_sum, *back),
            bytes_accessed=24 * rows * kv_width // PARTS,
        )
        owns.append(own_sum)
        lasts.append(along(before_sum, -reach))
    step = 1
    while step < reach:
        sink_row = sink_row + exchanged(sink_row, step)
        step *= 2
    grad_keys, grad_values, grad_sinks = kernel_call(
        functools.partial(finish_kernel, PARTS),
        [jax.ShapeDtypeStruct(keys.shape, BF16)] * 2 + [jax.ShapeDtypeStruct(sinks.shape, F32)],
        [VMEM] * (1 + 2 * PARTS),
        (sink_row, *owns, *lasts),
        bytes_accessed=16 * rows * kv_width,
    )
    return grad_queries[None], grad_keys[None], grad_values[None], grad_sinks


def solution(mesh):
    blocks = P("dp", "ctx", None)
    in_specs = (blocks, blocks, blocks, blocks, P(), P("dp", None))
    out_specs = (blocks, blocks, blocks, P())
    return jax.shard_map(local, mesh=mesh, in_specs=in_specs, out_specs=out_specs, check_vma=False)
```

```python
import functools

import jax
import jax.numpy as jnp
from jax import lax
from jax.experimental import pallas as pl
from jax.experimental.pallas import tpu as pltpu
from jax.sharding import PartitionSpec as P

WINDOW = 512
LOG2E = 1.4426950408889634

F32 = jnp.float32
BF16 = jnp.bfloat16
SMEM = pl.BlockSpec(memory_space=pltpu.SMEM)
VMEM = pl.BlockSpec(memory_space=pltpu.VMEM)


def dot_nt(a, b):
    return lax.dot_general(a, b, (((1,), (1,)), ((), ())), preferred_element_type=F32)


def dot_nn(a, b):
    return lax.dot_general(a, b, (((1,), (0,)), ((), ())), preferred_element_type=F32)


def dot_tn(a, b):
    return lax.dot_general(a, b, (((0,), (0,)), ((), ())), preferred_element_type=F32)


def kernel_call(body, out_shape, in_specs, operands):
    return pl.pallas_call(
        body,
        out_shape=out_shape,
        in_specs=in_specs,
        out_specs=[VMEM] * len(out_shape),
        compiler_params=pltpu.CompilerParams(vmem_limit_bytes=24 * 1024 * 1024),
        cost_estimate=pl.CostEstimate(flops=0, bytes_accessed=0, transcendentals=0),
    )(*operands)


def later(slot, step):
    return lax.bitwise_xor(slot, step) > slot


def choose(slot, own, before_ref, out_refs):
    for bit, ref in enumerate(out_refs):
        @pl.when(later(slot, 1 << bit))
        def _():
            ref[...] = own

        @pl.when(jnp.logical_not(later(slot, 1 << bit)))
        def _():
            ref[...] = before_ref[...]


def keys_kernel(reach, place_ref, own_ref, before_ref, *out_refs):
    choose(lax.rem(place_ref[0], reach), own_ref[:, :before_ref.shape[1]], before_ref, out_refs)


def tables_kernel(reach, rows, group, place_ref, docs_ref, sinks_ref, own_ref, before_ref, pair_ref, *refs):
    caps_ref, tops_ref, *out_refs = refs
    place = place_ref[0]
    slot = lax.rem(place, reach)
    choose(slot, own_ref[:, before_ref.shape[1]:], before_ref, out_refs)
    doc = docs_ref[0, place]
    columns = caps_ref.shape[1]
    for step in range(1, reach + 1):
        distance = reach
        if step < reach:
            distance = lax.rem(slot - lax.bitwise_xor(slot, step) + reach, reach)
        other = docs_ref[0, jnp.maximum(place - distance, 0)]
        same = jnp.logical_and(place >= distance, other == doc)
        caps_ref[step:step + 1, :] = jnp.full((1, columns), jnp.where(same, jnp.inf, -jnp.inf), F32)
    for head in range(sinks_ref.shape[0] // group):
        for j in range(group):
            tops_ref[head:head + 1, j * rows:(j + 1) * rows] = jnp.full(
                (1, rows), sinks_ref[head * group + j] * LOG2E, F32
            )


def block(x, i, rows):
    return x[i * rows:(i + 1) * rows]


def causal_mask(rows, group):
    shape = (rows, group * rows)
    key_at = lax.broadcasted_iota(jnp.int32, shape, 0)
    return key_at <= lax.rem(lax.broadcasted_iota(jnp.int32, shape, 1), rows)


def parted(x, causal):
    zero = jnp.zeros((), x.dtype)
    return jnp.where(causal, x, zero), jnp.where(causal, zero, x)


def stacked(ref, first, group, size):
    return jnp.concatenate([ref[:, (first + j) * size:(first + j + 1) * size] for j in range(group)], axis=0)


def store_shares(x, cut, rows, reach, own_ref, before_ref, message_refs):
    own_ref[:, cut] = block(x, 0, rows)
    before_ref[:, cut] = block(x, reach, rows)
    for i, ref in enumerate(message_refs, 1):
        ref[:, cut] = block(x, i, rows).astype(BF16)


def probs_kernel(kv_heads, group, reach, rows, size, caps_ref, tops_ref, pair_ref, *refs):
    blocks = refs[:reach + 1]
    probs_ref, sink_ref, own_ref, before_ref, *message_refs = refs[reach + 1:]
    to_log2 = size ** (-0.5) * LOG2E
    causal = causal_mask(rows, group)
    caps = [caps_ref[i:i + 1, :] for i in range(reach + 1)]
    for head in range(kv_heads):
        cut = slice(head * size, (head + 1) * size)
        q = stacked(pair_ref, head * group, group, size)
        g = stacked(pair_ref, (kv_heads + head) * group, group, size)
        keys = jnp.concatenate([r[:, cut] for r in blocks], axis=0)
        scores = dot_nt(keys, q)
        s_blocks = [
            jnp.where(causal, block(scores, 0, rows), jnp.minimum(block(scores, reach, rows), caps[reach]))
        ] + [block(scores, i, rows) for i in range(1, reach)]
        top = tops_ref[head:head + 1, :]
        sink_log = top
        for i, s in enumerate(s_blocks):
            high = jnp.max(s, axis=0, keepdims=True) * to_log2
            top = jnp.maximum(top, jnp.minimum(high, caps[i]) if i else high)
        sink_weight = jnp.exp2(sink_log - top)
        summed = sink_weight
        raised = []
        for i, s in enumerate(s_blocks):
            e = jnp.exp2(s * to_log2 - (jnp.maximum(top, -caps[i]) if i else top))
            summed = summed + jnp.sum(e, axis=0, keepdims=True)
            raised.append(e)
        inverse = 1.0 / summed
        probs = [(e * inverse).astype(BF16) for e in raised]
        for i, p in enumerate(probs):
            at = (head * reach + i) * rows
            probs_ref[at:at + rows, :] = p
        sink_ref[head:head + 1, :] = sink_weight * inverse
        first, last = parted(probs[0], causal)
        dv = dot_nn(jnp.concatenate([first] + probs[1:] + [last], axis=0), g)
        store_shares(dv, cut, rows, reach, own_ref, before_ref, message_refs)


def scores_kernel(kv_heads, group, reach, rows, size, probs_ref, sinkp_ref, pair_ref, *refs):
    blocks = refs[:reach + 1]
    gscores_ref, sink_ref, own_ref, before_ref, *message_refs = refs[reach + 1:]
    scale = size ** (-0.5)
    columns = group * rows
    causal = causal_mask(rows, group)
    lane = lax.broadcasted_iota(jnp.int32, (1, 128), 1)
    sink_row = jnp.zeros((1, 128), F32)
    for head in range(kv_heads):
        cut = slice(head * size, (head + 1) * size)
        q = stacked(pair_ref, head * group, group, size)
        g = stacked(pair_ref, (kv_heads + head) * group, group, size)
        own_cut = slice((kv_heads + head) * size, (kv_heads + head + 1) * size)
        values = jnp.concatenate([blocks[0][:, own_cut]] + [r[:, cut] for r in blocks[1:]], axis=0)
        gprobs = dot_nt(values, g)
        t_blocks = [jnp.where(causal, block(gprobs, 0, rows), block(gprobs, reach, rows))]
        t_blocks += [block(gprobs, i, rows) for i in range(1, reach)]
        probs = [
            probs_ref[(head * reach + i) * rows:(head * reach + i + 1) * rows, :].astype(F32) for i in range(reach)
        ]
        delta = jnp.zeros((1, columns), F32)
        for p, t in zip(probs, t_blocks):
            delta = delta + jnp.sum(p * t, axis=0, keepdims=True)
        gscores = [(p * (t - delta)).astype(BF16) for p, t in zip(probs, t_blocks)]
        first, last = parted(gscores[0], causal)
        gscores = jnp.concatenate([first] + gscores[1:] + [last], axis=0)
        span = (reach + 1) * rows
        gscores_ref[head * span:(head + 1) * span, :] = gscores
        dk = dot_nn(gscores, q) * scale
        store_shares(dk, cut, rows, reach, own_ref, before_ref, message_refs)
        sink_terms = sinkp_ref[head:head + 1, :] * delta
        for j in range(group):
            term = jnp.sum(sink_terms[:, j * rows:(j + 1) * rows], axis=1, keepdims=True)
            sink_row = jnp.where(lane == head * group + j, -term, sink_row)
    sink_ref[...] = sink_row


def queries_kernel(kv_heads, group, reach, rows, size, gscores_ref, *refs):
    *blocks, dq_ref, done_ref = refs
    scale = size ** (-0.5)
    span = (reach + 1) * rows
    for head in range(kv_heads):
        cut = slice(head * size, (head + 1) * size)
        keys = jnp.concatenate([r[:, cut] for r in blocks], axis=0)
        dq = (dot_tn(gscores_ref[head * span:(head + 1) * span, :], keys) * scale).astype(BF16)
        for j in range(group):
            at = (head * group + j) * size
            dq_ref[:, at:at + size] = dq[j * rows:(j + 1) * rows]
    done_ref[...] = jnp.zeros_like(done_ref)


def combine_kernel(reach, place_ref, own_ref, before_ref, *refs):
    *messages, own_out, before_out, done_ref = refs
    slot = lax.rem(place_ref[0], reach)
    own, before = own_ref[...], before_ref[...]
    for step, message in enumerate(messages, 1):
        mine = later(slot, step)
        back = message[...].astype(F32)
        own = own + jnp.where(mine, back, 0.0)
        before = before + jnp.where(mine, 0.0, back)
    own_out[...] = own
    before_out[...] = before.astype(BF16)
    done_ref[...] = jnp.zeros_like(done_ref)


def joined_kernel(share_ref, sink_ref, done_ref, share_out, sink_out):
    share_out[...] = share_ref[...]
    sink_out[...] = sink_ref[...] + done_ref[...]


def out_kernel(keys_ref, sink_ref, done_ref, keys_out, sink_out):
    keys_out[...] = keys_ref[...]
    sink_out[...] = sink_ref[0, :sink_out.shape[0]]


def total_kernel(own_ref, last_ref, out_ref):
    out_ref[...] = (own_ref[...] + last_ref[...].astype(F32)).astype(BF16)


def end_kernel(own_ref, last_ref, out_ref, done_ref):
    done_ref[...] = jnp.zeros_like(done_ref)
    out_ref[...] = (own_ref[...] + last_ref[...].astype(F32)).astype(BF16)


def local(queries, keys, values, grad_out, sinks, doc_ids):
    rows, q_width = queries.shape[1:]
    kv_width = keys.shape[2]
    heads = sinks.shape[0]
    size = q_width // heads
    group = q_width // kv_width
    kv_heads = kv_width // size
    reach = WINDOW // rows
    count = lax.axis_size("ctx")
    place = jnp.full((1,), lax.axis_index("ctx"), jnp.int32)
    queries, keys, values, grad_out = queries[0], keys[0], values[0], grad_out[0]
    wide = jax.ShapeDtypeStruct(keys.shape, F32)
    narrow = jax.ShapeDtypeStruct(keys.shape, BF16)
    row = jax.ShapeDtypeStruct((1, 128), F32)
    columns = group * rows
    table = jax.ShapeDtypeStruct((8 * (-(-max(reach + 1, kv_heads) // 8)), columns), F32)
    sizes = (kv_heads, group, reach, rows, size)

    def along(x, distance):
        if distance < 0:
            return lax.ppermute(x, "ctx", [(i, (i + distance) % count) for i in range(count)])
        first, last = max(0, -distance), min(count, count - distance)
        return lax.ppermute(x, "ctx", [(i, i + distance) for i in range(first, last)])

    def exchanged(x, step, axis="ctx"):
        return lax.ppermute(x, axis, [(i, i ^ step) for i in range(lax.axis_size(axis))])

    def summed_over(x, first, end):
        while first < end:
            x = x + exchanged(x, first)
            first *= 2
        return x

    keys_before = along(keys, reach)
    values_before = along(values, reach)
    own = jnp.concatenate([keys, values], axis=1)
    pair = jnp.concatenate([queries, grad_out], axis=1)

    def gathered(own, chosen, before):
        return [own, *(exchanged(chosen[step.bit_length() - 1], step) for step in range(1, reach)), before]

    choices = [narrow] * (reach.bit_length() - 1)
    chosen = kernel_call(
        functools.partial(keys_kernel, reach), choices, [SMEM, VMEM, VMEM], (place, own, keys_before)
    )
    key_blocks = gathered(own, chosen, keys_before)
    caps, tops, *chosen = kernel_call(
        functools.partial(tables_kernel, reach, rows, group),
        [table, table] + choices,
        [SMEM] * 3 + [VMEM] * 3,
        (place, doc_ids, sinks, own, values_before, pair),
    )
    value_blocks = gathered(own, chosen, values_before)
    probs, sink_probs, values_own, values_share, *messages = kernel_call(
        functools.partial(probs_kernel, *sizes),
        [jax.ShapeDtypeStruct((kv_heads * reach * rows, columns), BF16), table, wide, wide] + [narrow] * (reach - 1),
        [VMEM] * (4 + reach),
        (caps, tops, pair, *key_blocks),
    )
    values_back = [exchanged(m, step) for step, m in enumerate(messages, 1)]
    gscores, sink_row, keys_own, keys_share, *messages = kernel_call(
        functools.partial(scores_kernel, *sizes),
        [jax.ShapeDtypeStruct((kv_heads * (reach + 1) * rows, columns), BF16), row, wide, wide]
        + [narrow] * (reach - 1),
        [VMEM] * (4 + reach),
        (probs, sink_probs, pair, *value_blocks),
    )
    keys_back = [exchanged(m, step) for step, m in enumerate(messages, 1)]
    grad_queries, dq_done = kernel_call(
        functools.partial(queries_kernel, *sizes),
        [jax.ShapeDtypeStruct(queries.shape, BF16), row],
        [VMEM] * (2 + reach),
        (gscores, *key_blocks),
    )

    def combined(own, share, back):
        return kernel_call(
            functools.partial(combine_kernel, reach),
            [wide, narrow, row],
            [SMEM] + [VMEM] * (reach + 1),
            (place, own, share, *back),
        )

    values_own, values_share, done = combined(values_own, values_share, values_back)
    values_last = along(values_share, -reach)
    sink_row = sink_row + done
    if lax.axis_size("dp") == 2:
        sink_row = sink_row + exchanged(sink_row, 1, "dp")
    else:
        sink_row = lax.psum(sink_row, "dp")
    sink_row = summed_over(sink_row, reach, count)
    keys_own, keys_share, _ = combined(keys_own, keys_share, keys_back)
    keys_share, sink_row = kernel_call(
        joined_kernel, [narrow, row], [VMEM] * 3, (keys_share, sink_row, dq_done)
    )
    keys_last = along(keys_share, -reach)
    grad_values, done = kernel_call(end_kernel, [narrow, row], [VMEM] * 2, (values_own, values_last))
    sink_row = sink_row + exchanged(sink_row, 1) + done
    sink_row = summed_over(sink_row, 2, reach)
    grad_keys, = kernel_call(total_kernel, [narrow], [VMEM] * 2, (keys_own, keys_last))
    grad_keys, grad_sinks = kernel_call(
        out_kernel,
        [narrow, jax.ShapeDtypeStruct(sinks.shape, F32)],
        [VMEM] * 3,
        (grad_keys, sink_row, done),
    )
    return grad_queries[None], grad_keys[None], grad_values[None], grad_sinks


def solution(mesh):
    blocks = P("dp", "ctx", None)
    in_specs = (blocks, blocks, blocks, blocks, P(), P("dp", None))
    out_specs = (blocks, blocks, blocks, P())
    return jax.shard_map(local, mesh=mesh, in_specs=in_specs, out_specs=out_specs, check_vma=False)
```

```python
import functools

import jax
import jax.numpy as jnp
from jax import lax
from jax.experimental import pallas as pl
from jax.experimental.pallas import tpu as pltpu
from jax.sharding import PartitionSpec as P

WINDOW = 512
LOG2E = 1.4426950408889634
TERM_ROWS = 16

F32 = jnp.float32
BF16 = jnp.bfloat16
SMEM = pl.BlockSpec(memory_space=pltpu.SMEM)
VMEM = pl.BlockSpec(memory_space=pltpu.VMEM)


def dot_nt(a, b):
    return lax.dot_general(a, b, (((1,), (1,)), ((), ())), preferred_element_type=F32)


def dot_nn(a, b):
    return lax.dot_general(a, b, (((1,), (0,)), ((), ())), preferred_element_type=F32)


def dot_tn(a, b):
    return lax.dot_general(a, b, (((0,), (0,)), ((), ())), preferred_element_type=F32)


def kernel_call(body, out_shape, in_specs, operands, flops=0):
    return pl.pallas_call(
        body,
        out_shape=out_shape,
        in_specs=in_specs,
        out_specs=[VMEM] * len(out_shape),
        compiler_params=pltpu.CompilerParams(vmem_limit_bytes=24 * 1024 * 1024),
        cost_estimate=pl.CostEstimate(flops=flops, bytes_accessed=0, transcendentals=0),
    )(*operands)


def later(slot, step):
    return lax.bitwise_xor(slot, step) > slot


def choose(slot, own, before_ref, out_refs):
    for step, ref in enumerate(out_refs, 1):
        @pl.when(later(slot, step))
        def _():
            ref[...] = own

        @pl.when(jnp.logical_not(later(slot, step)))
        def _():
            ref[...] = before_ref[...]


def keys_kernel(reach, place_ref, own_ref, before_ref, *out_refs):
    choose(lax.rem(place_ref[0], reach), own_ref[:, :before_ref.shape[1]], before_ref, out_refs)


def tables_kernel(reach, rows, group, place_ref, docs_ref, sinks_ref, own_ref, before_ref, pair_ref, *refs):
    caps_ref, tops_ref, *out_refs = refs
    place = place_ref[0]
    slot = lax.rem(place, reach)
    choose(slot, own_ref[:, before_ref.shape[1]:], before_ref, out_refs)
    doc = docs_ref[0, place]
    columns = caps_ref.shape[1]
    for step in range(1, reach + 1):
        distance = reach
        if step < reach:
            distance = lax.rem(slot - lax.bitwise_xor(slot, step) + reach, reach)
        other = docs_ref[0, jnp.maximum(place - distance, 0)]
        same = jnp.logical_and(place >= distance, other == doc)
        caps_ref[step:step + 1, :] = jnp.full((1, columns), jnp.where(same, jnp.inf, -jnp.inf), F32)
    for head in range(sinks_ref.shape[0] // group):
        for j in range(group):
            tops_ref[head:head + 1, j * rows:(j + 1) * rows] = jnp.full(
                (1, rows), sinks_ref[head * group + j] * LOG2E, F32
            )


def block(x, i, rows):
    return x[i * rows:(i + 1) * rows]


def causal_mask(rows, group):
    shape = (rows, group * rows)
    key_at = lax.broadcasted_iota(jnp.int32, shape, 0)
    return key_at <= lax.rem(lax.broadcasted_iota(jnp.int32, shape, 1), rows)


def parted(x, causal):
    zero = jnp.zeros((), x.dtype)
    return jnp.where(causal, x, zero), jnp.where(causal, zero, x)


def split_terms(row):
    parts = []
    for _ in range(3):
        parts.append(row.astype(BF16))
        row = row - parts[-1].astype(F32)
    return jnp.concatenate(parts + [jnp.zeros((TERM_ROWS - 3, row.shape[1]), BF16)], axis=0)


def joined_terms(terms):
    parts = terms.astype(F32)
    return (parts[2:3] + parts[1:2]) + parts[0:1]


def stacked(ref, first, group, size):
    return jnp.concatenate([ref[:, (first + j) * size:(first + j + 1) * size] for j in range(group)], axis=0)


def store_shares(x, head, rows, reach, own_ref, before_ref, message_refs):
    at = slice(head * rows, (head + 1) * rows)
    own_ref[at, :] = block(x, 0, rows)
    before_ref[at, :] = block(x, reach, rows)
    for i, ref in enumerate(message_refs, 1):
        ref[at, :] = block(x, i, rows).astype(BF16)


def probs_kernel(kv_heads, group, reach, rows, size, caps_ref, tops_ref, pair_ref, *refs):
    blocks = refs[:reach + 1]
    probs_ref, sink_ref, own_ref, before_ref, *message_refs = refs[reach + 1:]
    to_log2 = size ** (-0.5) * LOG2E
    causal = causal_mask(rows, group)
    caps = [caps_ref[i:i + 1, :] for i in range(reach + 1)]
    for head in range(kv_heads):
        cut = slice(head * size, (head + 1) * size)
        q = stacked(pair_ref, head * group, group, size)
        g = stacked(pair_ref, (kv_heads + head) * group, group, size)
        keys = jnp.concatenate([r[:, cut] for r in blocks], axis=0)
        scores = dot_nt(keys, q)
        s_blocks = [
            jnp.where(causal, block(scores, 0, rows), jnp.minimum(block(scores, reach, rows), caps[reach]))
        ] + [block(scores, i, rows) for i in range(1, reach)]
        top = tops_ref[head:head + 1, :]
        sink_log = top
        for i, s in enumerate(s_blocks):
            high = jnp.max(s, axis=0, keepdims=True) * to_log2
            top = jnp.maximum(top, jnp.minimum(high, caps[i]) if i else high)
        sink_weight = jnp.exp2(sink_log - top)
        summed = sink_weight
        raised = []
        for i, s in enumerate(s_blocks):
            e = jnp.exp2(s * to_log2 - (jnp.maximum(top, -caps[i]) if i else top))
            summed = summed + jnp.sum(e, axis=0, keepdims=True)
            raised.append(e)
        inverse = 1.0 / summed
        probs = [(e * inverse).astype(BF16) for e in raised]
        for i, p in enumerate(probs):
            at = (head * reach + i) * rows
            probs_ref[at:at + rows, :] = p
        sink_ref[head:head + 1, :] = sink_weight * inverse
        first, last = parted(probs[0], causal)
        dv = dot_nn(jnp.concatenate([first] + probs[1:] + [last], axis=0), g)
        store_shares(dv, head, rows, reach, own_ref, before_ref, message_refs)


def scores_kernel(kv_heads, group, reach, rows, size, probs_ref, sinkp_ref, pair_ref, *refs):
    blocks = refs[:reach + 1]
    gscores_ref, sink_ref, own_ref, before_ref, *message_refs = refs[reach + 1:]
    scale = size ** (-0.5)
    columns = group * rows
    causal = causal_mask(rows, group)
    lane = lax.broadcasted_iota(jnp.int32, (1, 128), 1)
    sink_row = jnp.zeros((1, 128), F32)
    for head in range(kv_heads):
        cut = slice(head * size, (head + 1) * size)
        q = stacked(pair_ref, head * group, group, size)
        g = stacked(pair_ref, (kv_heads + head) * group, group, size)
        own_cut = slice((kv_heads + head) * size, (kv_heads + head + 1) * size)
        values = jnp.concatenate([blocks[0][:, own_cut]] + [r[:, cut] for r in blocks[1:]], axis=0)
        gprobs = dot_nt(values, g)
        t_blocks = [jnp.where(causal, block(gprobs, 0, rows), block(gprobs, reach, rows))]
        t_blocks += [block(gprobs, i, rows) for i in range(1, reach)]
        probs = [
            probs_ref[(head * reach + i) * rows:(head * reach + i + 1) * rows, :].astype(F32) for i in range(reach)
        ]
        delta = jnp.zeros((1, columns), F32)
        for p, t in zip(probs, t_blocks):
            delta = delta + jnp.sum(p * t, axis=0, keepdims=True)
        gscores = [(p * (t - delta)).astype(BF16) for p, t in zip(probs, t_blocks)]
        first, last = parted(gscores[0], causal)
        gscores = jnp.concatenate([first] + gscores[1:] + [last], axis=0)
        span = (reach + 1) * rows
        gscores_ref[head * span:(head + 1) * span, :] = gscores
        dk = dot_nn(gscores, q) * scale
        store_shares(dk, head, rows, reach, own_ref, before_ref, message_refs)
        sink_terms = sinkp_ref[head:head + 1, :] * delta
        for j in range(group):
            term = jnp.sum(sink_terms[:, j * rows:(j + 1) * rows], axis=1, keepdims=True)
            sink_row = jnp.where(lane == head * group + j, -term, sink_row)
    sink_ref[...] = sink_row
    terms = split_terms(sink_row)
    for ref in message_refs:
        ref[kv_heads * rows:, :] = terms


def queries_kernel(kv_heads, group, reach, rows, size, gscores_ref, own_ref, last_ref, *refs):
    *blocks, dv_ref, dq_ref, done_ref = refs
    side_by_side(own_ref, last_ref[...], dv_ref)
    scale = size ** (-0.5)
    span = (reach + 1) * rows
    for head in range(kv_heads):
        cut = slice(head * size, (head + 1) * size)
        keys = jnp.concatenate([r[:, cut] for r in blocks], axis=0)
        dq = (dot_tn(gscores_ref[head * span:(head + 1) * span, :], keys) * scale).astype(BF16)
        for j in range(group):
            at = (head * group + j) * size
            dq_ref[:, at:at + size] = dq[j * rows:(j + 1) * rows]
    done_ref[...] = jnp.zeros_like(done_ref)


def combine(reach, place_ref, own_ref, before_ref, messages, own_out, before_out):
    slot = lax.rem(place_ref[0], reach)
    own, before = own_ref[...], before_ref[...]
    for step, message in enumerate(messages, 1):
        mine = later(slot, step)
        back = message[:own.shape[0], :].astype(F32)
        own = own + jnp.where(mine, back, 0.0)
        before = before + jnp.where(mine, 0.0, back)
    own_out[...] = own
    before_out[...] = before.astype(BF16)


def values_kernel(reach, place_ref, own_ref, before_ref, *refs):
    *messages, own_out, before_out = refs
    combine(reach, place_ref, own_ref, before_ref, messages, own_out, before_out)


def sums_kernel(reach, place_ref, own_ref, before_ref, sink_ref, *refs):
    *messages, own_out, before_out, sink_out = refs
    height = own_ref.shape[0]
    combine(reach, place_ref, own_ref, before_ref, messages, own_out, before_out.at[:height, :])
    sink_row = sink_ref[...]
    for message in messages:
        sink_row = sink_row + joined_terms(message[height:, :])
    before_out[height:, :] = split_terms(sink_row)
    sink_out[...] = sink_row


def side_by_side(own_ref, last, out_ref):
    rows, width = out_ref.shape
    total = own_ref[...] + last.astype(F32)
    size = total.shape[1]
    for head in range(width // size):
        out_ref[:, head * size:(head + 1) * size] = block(total, head, rows).astype(BF16)


def totals_kernel(own_ref, last_ref, sink_ref, *refs):
    *sink_refs, keys_out, sink_out = refs
    height = own_ref.shape[0]
    side_by_side(own_ref, last_ref[:height, :], keys_out)
    sink_row = sink_ref[...] + joined_terms(last_ref[height:, :])
    for ref in sink_refs:
        sink_row = sink_row + ref[...]
    sink_out[...] = sink_row


def out_kernel(keys_ref, sink_ref, keys_out, sink_out):
    keys_out[...] = keys_ref[...]
    sink_out[...] = sink_ref[0, :sink_out.shape[0]]


def local(queries, keys, values, grad_out, sinks, doc_ids):
    rows, q_width = queries.shape[1:]
    kv_width = keys.shape[2]
    heads = sinks.shape[0]
    size = q_width // heads
    group = q_width // kv_width
    kv_heads = kv_width // size
    reach = WINDOW // rows
    count = lax.axis_size("ctx")
    place = jnp.full((1,), lax.axis_index("ctx"), jnp.int32)
    queries, keys, values, grad_out = queries[0], keys[0], values[0], grad_out[0]
    narrow = jax.ShapeDtypeStruct(keys.shape, BF16)
    wide = jax.ShapeDtypeStruct((kv_heads * rows, size), F32)
    share = jax.ShapeDtypeStruct(wide.shape, BF16)
    message = jax.ShapeDtypeStruct((kv_heads * rows + TERM_ROWS, size), BF16)
    row = jax.ShapeDtypeStruct((1, 128), F32)
    columns = group * rows
    table = jax.ShapeDtypeStruct((8 * (-(-max(reach + 1, kv_heads) // 8)), columns), F32)
    sizes = (kv_heads, group, reach, rows, size)
    span = (reach + 1) * rows

    def along(x, distance):
        return lax.ppermute(x, "ctx", [(i, (i + distance) % count) for i in range(count)])

    def exchanged(x, step, axis="ctx"):
        return lax.ppermute(x, axis, [(i, i ^ step) for i in range(lax.axis_size(axis))])

    keys_before = along(keys, reach)
    values_before = along(values, reach)
    own = jnp.concatenate([keys, values], axis=1)
    pair = jnp.concatenate([queries, grad_out], axis=1)

    def gathered(own, chosen, before):
        arrived = [exchanged(chosen[step - 1], step) for step in range(1, reach)]
        return [own, *arrived, before]

    choices = [narrow] * (reach - 1)
    chosen = kernel_call(
        functools.partial(keys_kernel, reach), choices, [SMEM, VMEM, VMEM], (place, own, keys_before)
    )
    key_blocks = gathered(own, chosen, keys_before)
    caps, tops, *chosen = kernel_call(
        functools.partial(tables_kernel, reach, rows, group),
        [table, table] + choices,
        [SMEM] * 3 + [VMEM] * 3,
        (place, doc_ids, sinks, own, values_before, pair),
    )
    value_blocks = gathered(own, chosen, values_before)
    probs, sink_probs, values_own, values_share, *messages = kernel_call(
        functools.partial(probs_kernel, *sizes),
        [jax.ShapeDtypeStruct((kv_heads * reach * rows, columns), BF16), table, wide, wide] + [share] * (reach - 1),
        [VMEM] * (4 + reach),
        (caps, tops, pair, *key_blocks),
    )
    values_back = [exchanged(m, step) for step, m in enumerate(messages, 1)]
    gscores, sink_row, keys_own, keys_share, *messages = kernel_call(
        functools.partial(scores_kernel, *sizes),
        [jax.ShapeDtypeStruct((kv_heads * (reach + 1) * rows, columns), BF16), row, wide, wide]
        + [message] * (reach - 1),
        [VMEM] * (4 + reach),
        (probs, sink_probs, pair, *value_blocks),
    )
    keys_back = [exchanged(m, step) for step, m in enumerate(messages, 1)]
    values_own, values_share = kernel_call(
        functools.partial(values_kernel, reach),
        [wide, share],
        [SMEM] + [VMEM] * (reach + 1),
        (place, values_own, values_share, *values_back),
    )
    values_last = along(values_share, -reach)
    keys_own, keys_share, sink_row = kernel_call(
        functools.partial(sums_kernel, reach),
        [wide, message, row],
        [SMEM] + [VMEM] * (reach + 2),
        (place, keys_own, keys_share, sink_row, *keys_back),
    )
    keys_last = along(keys_share, -reach)
    grad_values, grad_queries, done = kernel_call(
        functools.partial(queries_kernel, *sizes),
        [narrow, jax.ShapeDtypeStruct(queries.shape, BF16), row],
        [VMEM] * (4 + reach),
        (gscores, values_own, values_last, *key_blocks),
        2 * rows * group * span * size * kv_heads,
    )
    sink_rows = [sink_row] + [along(sink_row, -distance) for distance in range(2 * reach, count, reach)]
    sink_rows.append(done)
    grad_keys, sink_row = kernel_call(
        totals_kernel,
        [narrow, row],
        [VMEM] * (2 + len(sink_rows)),
        (keys_own, keys_last, *sink_rows),
    )
    if lax.axis_size("dp") == 2:
        sink_row = sink_row + exchanged(sink_row, 1, "dp")
    else:
        sink_row = lax.psum(sink_row, "dp")
    grad_keys, grad_sinks = kernel_call(
        out_kernel, [narrow, jax.ShapeDtypeStruct(sinks.shape, F32)], [VMEM] * 2, (grad_keys, sink_row)
    )
    return grad_queries[None], grad_keys[None], grad_values[None], grad_sinks


def solution(mesh):
    blocks = P("dp", "ctx", None)
    in_specs = (blocks, blocks, blocks, blocks, P(), P("dp", None))
    out_specs = (blocks, blocks, blocks, P())
    return jax.shard_map(local, mesh=mesh, in_specs=in_specs, out_specs=out_specs, check_vma=False)
```

```python
import functools

import jax
import jax.numpy as jnp
from jax import lax
from jax.experimental import pallas as pl
from jax.experimental.pallas import tpu as pltpu
from jax.sharding import PartitionSpec as P

WINDOW = 512
LOG2E = 1.4426950408889634
TERM_ROWS = 16

F32 = jnp.float32
BF16 = jnp.bfloat16
SMEM = pl.BlockSpec(memory_space=pltpu.SMEM)
VMEM = pl.BlockSpec(memory_space=pltpu.VMEM)


def dot_nt(a, b):
    return lax.dot_general(a, b, (((1,), (1,)), ((), ())), preferred_element_type=F32)


def dot_nn(a, b):
    return lax.dot_general(a, b, (((1,), (0,)), ((), ())), preferred_element_type=F32)


def dot_tn(a, b):
    return lax.dot_general(a, b, (((0,), (0,)), ((), ())), preferred_element_type=F32)


def kernel_call(body, out_shape, in_specs, operands, flops=0):
    return pl.pallas_call(
        body,
        out_shape=out_shape,
        in_specs=in_specs,
        out_specs=[VMEM] * len(out_shape),
        compiler_params=pltpu.CompilerParams(vmem_limit_bytes=24 * 1024 * 1024),
        cost_estimate=pl.CostEstimate(flops=flops, bytes_accessed=0, transcendentals=0),
    )(*operands)


def later(slot, step):
    return lax.bitwise_xor(slot, step) > slot


def choose(slot, own, before_ref, out_refs):
    for step, ref in enumerate(out_refs, 1):
        @pl.when(later(slot, step))
        def _():
            ref[...] = own

        @pl.when(jnp.logical_not(later(slot, step)))
        def _():
            ref[...] = before_ref[...]


def choose_kernel(reach, first, place_ref, own_ref, before_ref, *refs):
    width = before_ref.shape[1]
    choose(lax.rem(place_ref[0], reach), own_ref[:, first * width:(first + 1) * width], before_ref, refs[-(reach - 1):])


def tables_kernel(reach, rows, group, place_ref, docs_ref, sinks_ref, caps_ref, tops_ref):
    place = place_ref[0]
    slot = lax.rem(place, reach)
    doc = docs_ref[0, place]
    columns = caps_ref.shape[1]
    for step in range(1, reach + 1):
        distance = reach
        if step < reach:
            distance = lax.rem(slot - lax.bitwise_xor(slot, step) + reach, reach)
        other = docs_ref[0, jnp.maximum(place - distance, 0)]
        same = jnp.logical_and(place >= distance, other == doc)
        caps_ref[step:step + 1, :] = jnp.full((1, columns), jnp.where(same, jnp.inf, -jnp.inf), F32)
    for head in range(sinks_ref.shape[0] // group):
        for j in range(group):
            tops_ref[head:head + 1, j * rows:(j + 1) * rows] = jnp.full(
                (1, rows), sinks_ref[head * group + j] * LOG2E, F32
            )


def block(x, i, rows):
    return x[i * rows:(i + 1) * rows]


def causal_mask(rows, group):
    shape = (rows, group * rows)
    key_at = lax.broadcasted_iota(jnp.int32, shape, 0)
    return key_at <= lax.rem(lax.broadcasted_iota(jnp.int32, shape, 1), rows)


def parted(x, causal):
    zero = jnp.zeros((), x.dtype)
    return jnp.where(causal, x, zero), jnp.where(causal, zero, x)


def split_terms(row):
    parts = []
    for _ in range(3):
        parts.append(row.astype(BF16))
        row = row - parts[-1].astype(F32)
    return jnp.concatenate(parts + [jnp.zeros((TERM_ROWS - 3, row.shape[1]), BF16)], axis=0)


def joined_terms(terms):
    parts = terms.astype(F32)
    return (parts[2:3] + parts[1:2]) + parts[0:1]


def stacked(ref, first, group, size):
    return jnp.concatenate([ref[:, (first + j) * size:(first + j + 1) * size] for j in range(group)], axis=0)


def store_shares(x, head, rows, reach, own_ref, before_ref, message_refs):
    at = slice(head * rows, (head + 1) * rows)
    own_ref[at, :] = block(x, 0, rows)
    before_ref[at, :] = block(x, reach, rows)
    for i, ref in enumerate(message_refs, 1):
        ref[at, :] = block(x, i, rows).astype(BF16)


def softmax_part(s_blocks, caps, top, to_log2):
    sink_log = top
    for i, s in enumerate(s_blocks):
        high = jnp.max(s, axis=0, keepdims=True) * to_log2
        top = jnp.maximum(top, jnp.minimum(high, caps[i]) if i else high)
    sink_weight = jnp.exp2(sink_log - top)
    summed = sink_weight
    raised = []
    for i, s in enumerate(s_blocks):
        e = jnp.exp2(s * to_log2 - (jnp.maximum(top, -caps[i]) if i else top))
        summed = summed + jnp.sum(e, axis=0, keepdims=True)
        raised.append(e)
    inverse = 1.0 / summed
    probs = [(e * inverse).astype(BF16) for e in raised]
    return probs, sink_weight * inverse


def probs_kernel(kv_heads, group, reach, rows, size, caps_ref, tops_ref, pair_ref, *refs):
    blocks = refs[:reach + 1]
    probs_ref, sink_ref, own_ref, before_ref, *message_refs = refs[reach + 1:]
    to_log2 = size ** (-0.5) * LOG2E
    causal = causal_mask(rows, group)
    caps = [caps_ref[i:i + 1, :] for i in range(reach + 1)]

    def scores_of(head):
        cut = slice(head * size, (head + 1) * size)
        q = stacked(pair_ref, head * group, group, size)
        keys = jnp.concatenate([r[:, cut] for r in blocks], axis=0)
        return dot_nt(keys, q)

    waiting = None
    following = scores_of(0)
    for head in range(kv_heads):
        g = stacked(pair_ref, (kv_heads + head) * group, group, size)
        scores = following
        if head + 1 < kv_heads:
            following = scores_of(head + 1)
        s_blocks = [
            jnp.where(causal, block(scores, 0, rows), jnp.minimum(block(scores, reach, rows), caps[reach]))
        ] + [block(scores, i, rows) for i in range(1, reach)]
        parts = []
        for chunk in range(2):
            at = slice(chunk * group * rows // 2, (chunk + 1) * group * rows // 2)
            parts.append(
                softmax_part(
                    [s[:, at] for s in s_blocks], [c[:, at] for c in caps], tops_ref[head:head + 1, at], to_log2
                )
            )
        probs = [jnp.concatenate([p[0][i] for p in parts], axis=1) for i in range(reach)]
        sinkp = jnp.concatenate([p[1] for p in parts], axis=1)
        for i, p in enumerate(probs):
            at = (head * reach + i) * rows
            probs_ref[at:at + rows, :] = p
        sink_ref[head:head + 1, :] = sinkp
        first, last = parted(probs[0], causal)
        if waiting is not None:
            store_shares(dot_nn(*waiting), head - 1, rows, reach, own_ref, before_ref, message_refs)
        waiting = (jnp.concatenate([first] + probs[1:] + [last], axis=0), g)
    store_shares(dot_nn(*waiting), kv_heads - 1, rows, reach, own_ref, before_ref, message_refs)


def scores_kernel(kv_heads, group, reach, rows, size, probs_ref, sinkp_ref, pair_ref, *refs):
    blocks = refs[:reach + 1]
    gscores_ref, sink_ref, own_ref, before_ref, *message_refs = refs[reach + 1:]
    scale = size ** (-0.5)
    columns = group * rows
    causal = causal_mask(rows, group)
    lane = lax.broadcasted_iota(jnp.int32, (1, 128), 1)
    sink_row = jnp.zeros((1, 128), F32)

    def gprobs_of(head):
        cut = slice(head * size, (head + 1) * size)
        g = stacked(pair_ref, (kv_heads + head) * group, group, size)
        own_cut = slice((kv_heads + head) * size, (kv_heads + head + 1) * size)
        values = jnp.concatenate([blocks[0][:, own_cut]] + [r[:, cut] for r in blocks[1:]], axis=0)
        return dot_nt(values, g)

    waiting = None
    following = gprobs_of(0)
    for head in range(kv_heads):
        q = stacked(pair_ref, head * group, group, size)
        gprobs = following
        if head + 1 < kv_heads:
            following = gprobs_of(head + 1)
        t_blocks = [jnp.where(causal, block(gprobs, 0, rows), block(gprobs, reach, rows))]
        t_blocks += [block(gprobs, i, rows) for i in range(1, reach)]
        probs = [
            probs_ref[(head * reach + i) * rows:(head * reach + i + 1) * rows, :].astype(F32) for i in range(reach)
        ]
        delta = jnp.zeros((1, columns), F32)
        for p, t in zip(probs, t_blocks):
            delta = delta + jnp.sum(p * t, axis=0, keepdims=True)
        gscores = [(p * (t - delta)).astype(BF16) for p, t in zip(probs, t_blocks)]
        first, last = parted(gscores[0], causal)
        gscores = jnp.concatenate([first] + gscores[1:] + [last], axis=0)
        span = (reach + 1) * rows
        gscores_ref[head * span:(head + 1) * span, :] = gscores
        if waiting is not None:
            store_shares(dot_nn(*waiting) * scale, head - 1, rows, reach, own_ref, before_ref, message_refs)
        waiting = (gscores, q)
        sink_terms = sinkp_ref[head:head + 1, :] * delta
        for j in range(group):
            term = jnp.sum(sink_terms[:, j * rows:(j + 1) * rows], axis=1, keepdims=True)
            sink_row = jnp.where(lane == head * group + j, -term, sink_row)
    store_shares(dot_nn(*waiting) * scale, kv_heads - 1, rows, reach, own_ref, before_ref, message_refs)
    sink_ref[...] = sink_row
    terms = split_terms(sink_row)
    for ref in message_refs:
        ref[kv_heads * rows:, :] = terms


def queries_kernel(kv_heads, group, reach, rows, size, gscores_ref, own_ref, last_ref, *refs):
    *blocks, dv_ref, dq_ref, done_ref = refs
    side_by_side(own_ref, last_ref[...], dv_ref)
    scale = size ** (-0.5)
    span = (reach + 1) * rows
    for head in range(kv_heads):
        cut = slice(head * size, (head + 1) * size)
        keys = jnp.concatenate([r[:, cut] for r in blocks], axis=0)
        dq = (dot_tn(gscores_ref[head * span:(head + 1) * span, :], keys) * scale).astype(BF16)
        for j in range(group):
            at = (head * group + j) * size
            dq_ref[:, at:at + size] = dq[j * rows:(j + 1) * rows]
    done_ref[...] = jnp.zeros_like(done_ref)


def combine(reach, place_ref, own_ref, before_ref, messages, own_out, before_out):
    slot = lax.rem(place_ref[0], reach)
    own, before = own_ref[...], before_ref[...]
    for step, message in enumerate(messages, 1):
        mine = later(slot, step)
        back = message[:own.shape[0], :].astype(F32)
        own = own + jnp.where(mine, back, 0.0)
        before = before + jnp.where(mine, 0.0, back)
    own_out[...] = own
    before_out[...] = before.astype(BF16)


def values_kernel(reach, place_ref, own_ref, before_ref, *refs):
    *messages, own_out, before_out = refs
    combine(reach, place_ref, own_ref, before_ref, messages, own_out, before_out)


def sums_kernel(reach, place_ref, own_ref, before_ref, sink_ref, *refs):
    *messages, own_out, before_out, sink_out = refs
    height = own_ref.shape[0]
    combine(reach, place_ref, own_ref, before_ref, messages, own_out, before_out.at[:height, :])
    sink_row = sink_ref[...]
    for message in messages:
        sink_row = sink_row + joined_terms(message[height:, :])
    before_out[height:, :] = split_terms(sink_row)
    sink_out[...] = sink_row


def side_by_side(own_ref, last, out_ref):
    rows, width = out_ref.shape
    total = own_ref[...] + last.astype(F32)
    size = total.shape[1]
    for head in range(width // size):
        out_ref[:, head * size:(head + 1) * size] = block(total, head, rows).astype(BF16)


def totals_kernel(own_ref, last_ref, sink_ref, *refs):
    *sink_refs, keys_out, sink_out = refs
    height = own_ref.shape[0]
    side_by_side(own_ref, last_ref[:height, :], keys_out)
    sink_row = sink_ref[...] + joined_terms(last_ref[height:, :])
    for ref in sink_refs:
        sink_row = sink_row + ref[...]
    sink_out[...] = sink_row


def out_kernel(keys_ref, sink_ref, keys_out, sink_out):
    keys_out[...] = keys_ref[...]
    sink_out[...] = sink_ref[0, :sink_out.shape[0]]


def local(queries, keys, values, grad_out, sinks, doc_ids):
    rows, q_width = queries.shape[1:]
    kv_width = keys.shape[2]
    heads = sinks.shape[0]
    size = q_width // heads
    group = q_width // kv_width
    kv_heads = kv_width // size
    reach = WINDOW // rows
    count = lax.axis_size("ctx")
    place = jnp.full((1,), lax.axis_index("ctx"), jnp.int32)
    queries, keys, values, grad_out = queries[0], keys[0], values[0], grad_out[0]
    narrow = jax.ShapeDtypeStruct(keys.shape, BF16)
    wide = jax.ShapeDtypeStruct((kv_heads * rows, size), F32)
    share = jax.ShapeDtypeStruct(wide.shape, BF16)
    message = jax.ShapeDtypeStruct((kv_heads * rows + TERM_ROWS, size), BF16)
    row = jax.ShapeDtypeStruct((1, 128), F32)
    columns = group * rows
    table = jax.ShapeDtypeStruct((8 * (-(-max(reach + 1, kv_heads) // 8)), columns), F32)
    sizes = (kv_heads, group, reach, rows, size)
    span = (reach + 1) * rows

    def along(x, distance):
        return lax.ppermute(x, "ctx", [(i, (i + distance) % count) for i in range(count)])

    def exchanged(x, step, axis="ctx"):
        return lax.ppermute(x, axis, [(i, i ^ step) for i in range(lax.axis_size(axis))])

    keys_before = along(keys, reach)
    values_before = along(values, reach)
    own = jnp.concatenate([keys, values], axis=1)
    pair = jnp.concatenate([queries, grad_out], axis=1)

    def gathered(own, chosen, before):
        arrived = [exchanged(chosen[step - 1], step) for step in range(1, reach)]
        return [own, *arrived, before]

    caps, tops = kernel_call(
        functools.partial(tables_kernel, reach, rows, group), [table, table], [SMEM] * 3, (place, doc_ids, sinks)
    )
    choices = [narrow] * (reach - 1)
    chosen = kernel_call(
        functools.partial(choose_kernel, reach, 0),
        choices,
        [SMEM] + [VMEM] * 4,
        (place, own, keys_before, pair, caps),
    )
    key_blocks = gathered(own, chosen, keys_before)
    chosen = kernel_call(
        functools.partial(choose_kernel, reach, 1), choices, [SMEM] + [VMEM] * 2, (place, own, values_before)
    )
    value_blocks = gathered(own, chosen, values_before)
    probs, sink_probs, values_own, values_share, *messages = kernel_call(
        functools.partial(probs_kernel, *sizes),
        [jax.ShapeDtypeStruct((kv_heads * reach * rows, columns), BF16), table, wide, wide] + [share] * (reach - 1),
        [VMEM] * (4 + reach),
        (caps, tops, pair, *key_blocks),
    )
    values_back = [exchanged(m, step) for step, m in enumerate(messages, 1)]
    gscores, sink_row, keys_own, keys_share, *messages = kernel_call(
        functools.partial(scores_kernel, *sizes),
        [jax.ShapeDtypeStruct((kv_heads * (reach + 1) * rows, columns), BF16), row, wide, wide]
        + [message] * (reach - 1),
        [VMEM] * (4 + reach),
        (probs, sink_probs, pair, *value_blocks),
    )
    keys_back = [exchanged(m, step) for step, m in enumerate(messages, 1)]
    values_own, values_share = kernel_call(
        functools.partial(values_kernel, reach),
        [wide, share],
        [SMEM] + [VMEM] * (reach + 1),
        (place, values_own, values_share, *values_back),
    )
    values_last = along(values_share, -reach)
    keys_own, keys_share, sink_row = kernel_call(
        functools.partial(sums_kernel, reach),
        [wide, message, row],
        [SMEM] + [VMEM] * (reach + 2),
        (place, keys_own, keys_share, sink_row, *keys_back),
    )
    keys_last = along(keys_share, -reach)
    grad_values, grad_queries, done = kernel_call(
        functools.partial(queries_kernel, *sizes),
        [narrow, jax.ShapeDtypeStruct(queries.shape, BF16), row],
        [VMEM] * (4 + reach),
        (gscores, values_own, values_last, *key_blocks),
        2 * rows * group * span * size * kv_heads,
    )
    sink_rows = [sink_row] + [along(sink_row, -distance) for distance in range(2 * reach, count, reach)]
    sink_rows.append(done)
    grad_keys, sink_row = kernel_call(
        totals_kernel,
        [narrow, row],
        [VMEM] * (2 + len(sink_rows)),
        (keys_own, keys_last, *sink_rows),
    )
    if lax.axis_size("dp") == 2:
        sink_row = sink_row + exchanged(sink_row, 1, "dp")
    else:
        sink_row = lax.psum(sink_row, "dp")
    grad_keys, grad_sinks = kernel_call(
        out_kernel, [narrow, jax.ShapeDtypeStruct(sinks.shape, F32)], [VMEM] * 2, (grad_keys, sink_row)
    )
    return grad_queries[None], grad_keys[None], grad_values[None], grad_sinks


def solution(mesh):
    blocks = P("dp", "ctx", None)
    in_specs = (blocks, blocks, blocks, blocks, P(), P("dp", None))
    out_specs = (blocks, blocks, blocks, P())
    return jax.shard_map(local, mesh=mesh, in_specs=in_specs, out_specs=out_specs, check_vma=False)
```

```python
import functools

import jax
import jax.numpy as jnp
from jax import lax
from jax.experimental import pallas as pl
from jax.experimental.pallas import tpu as pltpu
from jax.sharding import PartitionSpec as P

WINDOW = 512
LOG2E = 1.4426950408889634
TERM_ROWS = 16

F32 = jnp.float32
BF16 = jnp.bfloat16
SMEM = pl.BlockSpec(memory_space=pltpu.SMEM)
VMEM = pl.BlockSpec(memory_space=pltpu.VMEM)


def dot_nt(a, b):
    return lax.dot_general(a, b, (((1,), (1,)), ((), ())), preferred_element_type=F32)


def dot_nn(a, b):
    return lax.dot_general(a, b, (((1,), (0,)), ((), ())), preferred_element_type=F32)


def dot_tn(a, b):
    return lax.dot_general(a, b, (((0,), (0,)), ((), ())), preferred_element_type=F32)


def kernel_call(body, out_shape, in_specs, operands, flops=0):
    return pl.pallas_call(
        body,
        out_shape=out_shape,
        in_specs=in_specs,
        out_specs=[VMEM] * len(out_shape),
        compiler_params=pltpu.CompilerParams(vmem_limit_bytes=24 * 1024 * 1024),
        cost_estimate=pl.CostEstimate(flops=flops, bytes_accessed=0, transcendentals=0),
    )(*operands)


def later(slot, step):
    return lax.bitwise_xor(slot, step) > slot


def choose(slot, own, before_ref, out_refs):
    for step, ref in enumerate(out_refs, 1):
        @pl.when(later(slot, step))
        def _():
            ref[...] = own

        @pl.when(jnp.logical_not(later(slot, step)))
        def _():
            ref[...] = before_ref[...]


def choose_kernel(reach, first, place_ref, own_ref, before_ref, *refs):
    width = before_ref.shape[1]
    choose(lax.rem(place_ref[0], reach), own_ref[:, first * width:(first + 1) * width], before_ref, refs[-(reach - 1):])


def tables_kernel(reach, rows, group, place_ref, docs_ref, sinks_ref, own_ref, caps_ref, tops_ref, values_ref):
    values_ref[...] = own_ref[:, values_ref.shape[1]:]
    place = place_ref[0]
    slot = lax.rem(place, reach)
    doc = docs_ref[0, place]
    columns = caps_ref.shape[1]
    for step in range(1, reach + 1):
        distance = reach
        if step < reach:
            distance = lax.rem(slot - lax.bitwise_xor(slot, step) + reach, reach)
        other = docs_ref[0, jnp.maximum(place - distance, 0)]
        same = jnp.logical_and(place >= distance, other == doc)
        caps_ref[step:step + 1, :] = jnp.full((1, columns), jnp.where(same, jnp.inf, -jnp.inf), F32)
    for head in range(sinks_ref.shape[0] // group):
        for j in range(group):
            tops_ref[head:head + 1, j * rows:(j + 1) * rows] = jnp.full(
                (1, rows), sinks_ref[head * group + j] * LOG2E, F32
            )


def block(x, i, rows):
    return x[i * rows:(i + 1) * rows]


def causal_mask(rows, group):
    shape = (rows, group * rows)
    key_at = lax.broadcasted_iota(jnp.int32, shape, 0)
    return key_at <= lax.rem(lax.broadcasted_iota(jnp.int32, shape, 1), rows)


def parted(x, causal):
    zero = jnp.zeros((), x.dtype)
    return jnp.where(causal, x, zero), jnp.where(causal, zero, x)


def split_terms(row):
    parts = []
    for _ in range(3):
        parts.append(row.astype(BF16))
        row = row - parts[-1].astype(F32)
    return jnp.concatenate(parts + [jnp.zeros((TERM_ROWS - 3, row.shape[1]), BF16)], axis=0)


def joined_terms(terms):
    parts = terms.astype(F32)
    return (parts[2:3] + parts[1:2]) + parts[0:1]


def stacked(ref, first, group, size):
    return jnp.concatenate([ref[:, (first + j) * size:(first + j + 1) * size] for j in range(group)], axis=0)


def store_shares(x, head, rows, reach, own_ref, before_ref, message_refs):
    at = slice(head * rows, (head + 1) * rows)
    own_ref[at, :] = block(x, 0, rows)
    before_ref[at, :] = block(x, reach, rows)
    for i, ref in enumerate(message_refs, 1):
        ref[at, :] = block(x, i, rows).astype(BF16)


def softmax_part(s_blocks, caps, top, to_log2):
    sink_log = top
    for i, s in enumerate(s_blocks):
        high = jnp.max(s, axis=0, keepdims=True) * to_log2
        top = jnp.maximum(top, jnp.minimum(high, caps[i]) if i else high)
    sink_weight = jnp.exp2(sink_log - top)
    summed = sink_weight
    raised = []
    for i, s in enumerate(s_blocks):
        e = jnp.exp2(s * to_log2 - (jnp.maximum(top, -caps[i]) if i else top))
        summed = summed + jnp.sum(e, axis=0, keepdims=True)
        raised.append(e)
    inverse = 1.0 / summed
    probs = [(e * inverse).astype(BF16) for e in raised]
    return probs, sink_weight * inverse


def probs_kernel(kv_heads, group, reach, rows, size, caps_ref, tops_ref, pair_ref, *refs):
    blocks = refs[:reach + 1]
    probs_ref, sink_ref, own_ref, before_ref, *message_refs = refs[reach + 1:]
    to_log2 = size ** (-0.5) * LOG2E
    causal = causal_mask(rows, group)
    caps = [caps_ref[i:i + 1, :] for i in range(reach + 1)]

    def scores_of(head):
        cut = slice(head * size, (head + 1) * size)
        q = stacked(pair_ref, head * group, group, size)
        keys = jnp.concatenate([r[:, cut] for r in blocks], axis=0)
        return dot_nt(keys, q)

    waiting = None
    following = scores_of(0)
    for head in range(kv_heads):
        g = stacked(pair_ref, (kv_heads + head) * group, group, size)
        scores = following
        if head + 1 < kv_heads:
            following = scores_of(head + 1)
        s_blocks = [
            jnp.where(causal, block(scores, 0, rows), jnp.minimum(block(scores, reach, rows), caps[reach]))
        ] + [block(scores, i, rows) for i in range(1, reach)]
        parts = []
        for chunk in range(2):
            at = slice(chunk * group * rows // 2, (chunk + 1) * group * rows // 2)
            parts.append(
                softmax_part(
                    [s[:, at] for s in s_blocks], [c[:, at] for c in caps], tops_ref[head:head + 1, at], to_log2
                )
            )
        probs = [jnp.concatenate([p[0][i] for p in parts], axis=1) for i in range(reach)]
        sinkp = jnp.concatenate([p[1] for p in parts], axis=1)
        for i, p in enumerate(probs):
            at = (head * reach + i) * rows
            probs_ref[at:at + rows, :] = p
        sink_ref[head:head + 1, :] = sinkp
        first, last = parted(probs[0], causal)
        if waiting is not None:
            store_shares(dot_nn(*waiting), head - 1, rows, reach, own_ref, before_ref, message_refs)
        waiting = (jnp.concatenate([first] + probs[1:] + [last], axis=0), g)
    store_shares(dot_nn(*waiting), kv_heads - 1, rows, reach, own_ref, before_ref, message_refs)


def scores_kernel(kv_heads, group, reach, rows, size, probs_ref, sinkp_ref, pair_ref, *refs):
    blocks = refs[:reach + 1]
    gscores_ref, sink_ref, own_ref, before_ref, *message_refs = refs[reach + 1:]
    scale = size ** (-0.5)
    columns = group * rows
    causal = causal_mask(rows, group)
    lane = lax.broadcasted_iota(jnp.int32, (1, 128), 1)
    sink_row = jnp.zeros((1, 128), F32)

    def gprobs_of(head):
        cut = slice(head * size, (head + 1) * size)
        g = stacked(pair_ref, (kv_heads + head) * group, group, size)
        own_cut = slice((kv_heads + head) * size, (kv_heads + head + 1) * size)
        values = jnp.concatenate([blocks[0][:, own_cut]] + [r[:, cut] for r in blocks[1:]], axis=0)
        return dot_nt(values, g)

    waiting = None
    following = gprobs_of(0)
    for head in range(kv_heads):
        q = stacked(pair_ref, head * group, group, size)
        gprobs = following
        if head + 1 < kv_heads:
            following = gprobs_of(head + 1)
        t_blocks = [jnp.where(causal, block(gprobs, 0, rows), block(gprobs, reach, rows))]
        t_blocks += [block(gprobs, i, rows) for i in range(1, reach)]
        probs = [
            probs_ref[(head * reach + i) * rows:(head * reach + i + 1) * rows, :].astype(F32) for i in range(reach)
        ]
        delta = jnp.zeros((1, columns), F32)
        for p, t in zip(probs, t_blocks):
            delta = delta + jnp.sum(p * t, axis=0, keepdims=True)
        gscores = [(p * (t - delta)).astype(BF16) for p, t in zip(probs, t_blocks)]
        first, last = parted(gscores[0], causal)
        gscores = jnp.concatenate([first] + gscores[1:] + [last], axis=0)
        span = (reach + 1) * rows
        gscores_ref[head * span:(head + 1) * span, :] = gscores
        if waiting is not None:
            store_shares(dot_nn(*waiting) * scale, head - 1, rows, reach, own_ref, before_ref, message_refs)
        waiting = (gscores, q)
        sink_terms = sinkp_ref[head:head + 1, :] * delta
        for j in range(group):
            term = jnp.sum(sink_terms[:, j * rows:(j + 1) * rows], axis=1, keepdims=True)
            sink_row = jnp.where(lane == head * group + j, -term, sink_row)
    store_shares(dot_nn(*waiting) * scale, kv_heads - 1, rows, reach, own_ref, before_ref, message_refs)
    sink_ref[...] = sink_row
    terms = split_terms(sink_row)
    for ref in message_refs:
        ref[kv_heads * rows:, :] = terms


def queries_kernel(kv_heads, group, reach, rows, size, gscores_ref, own_ref, last_ref, *refs):
    *blocks, dv_ref, dq_ref, done_ref = refs
    side_by_side(own_ref, last_ref[...], dv_ref)
    scale = size ** (-0.5)
    span = (reach + 1) * rows
    for head in range(kv_heads):
        cut = slice(head * size, (head + 1) * size)
        keys = jnp.concatenate([r[:, cut] for r in blocks], axis=0)
        dq = (dot_tn(gscores_ref[head * span:(head + 1) * span, :], keys) * scale).astype(BF16)
        for j in range(group):
            at = (head * group + j) * size
            dq_ref[:, at:at + size] = dq[j * rows:(j + 1) * rows]
    done_ref[...] = jnp.zeros_like(done_ref)


def combine(reach, place_ref, own_ref, before_ref, messages, own_out, before_out):
    slot = lax.rem(place_ref[0], reach)
    own, before = own_ref[...], before_ref[...]
    for step, message in enumerate(messages, 1):
        mine = later(slot, step)
        back = message[:own.shape[0], :].astype(F32)
        own = own + jnp.where(mine, back, 0.0)
        before = before + jnp.where(mine, 0.0, back)
    own_out[...] = own
    before_out[...] = before.astype(BF16)


def values_kernel(reach, place_ref, own_ref, before_ref, *refs):
    *messages, own_out, before_out = refs
    combine(reach, place_ref, own_ref, before_ref, messages, own_out, before_out)


def sums_kernel(reach, place_ref, own_ref, before_ref, sink_ref, *refs):
    *messages, own_out, before_out, sink_out = refs
    height = own_ref.shape[0]
    combine(reach, place_ref, own_ref, before_ref, messages, own_out, before_out.at[:height, :])
    sink_row = sink_ref[...]
    for message in messages:
        sink_row = sink_row + joined_terms(message[height:, :])
    before_out[height:, :] = split_terms(sink_row)
    sink_out[...] = sink_row


def side_by_side(own_ref, last, out_ref):
    rows, width = out_ref.shape
    total = own_ref[...] + last.astype(F32)
    size = total.shape[1]
    for head in range(width // size):
        out_ref[:, head * size:(head + 1) * size] = block(total, head, rows).astype(BF16)


def totals_kernel(own_ref, last_ref, sink_ref, *refs):
    *sink_refs, keys_out, sink_out = refs
    height = own_ref.shape[0]
    side_by_side(own_ref, last_ref[:height, :], keys_out)
    sink_row = sink_ref[...] + joined_terms(last_ref[height:, :])
    for ref in sink_refs:
        sink_row = sink_row + ref[...]
    sink_out[...] = sink_row


def out_kernel(keys_ref, sink_ref, keys_out, sink_out):
    keys_out[...] = keys_ref[...]
    sink_out[...] = sink_ref[0, :sink_out.shape[0]]


def local(queries, keys, values, grad_out, sinks, doc_ids):
    rows, q_width = queries.shape[1:]
    kv_width = keys.shape[2]
    heads = sinks.shape[0]
    size = q_width // heads
    group = q_width // kv_width
    kv_heads = kv_width // size
    reach = WINDOW // rows
    count = lax.axis_size("ctx")
    place = jnp.full((1,), lax.axis_index("ctx"), jnp.int32)
    queries, keys, values, grad_out = queries[0], keys[0], values[0], grad_out[0]
    narrow = jax.ShapeDtypeStruct(keys.shape, BF16)
    wide = jax.ShapeDtypeStruct((kv_heads * rows, size), F32)
    share = jax.ShapeDtypeStruct(wide.shape, BF16)
    message = jax.ShapeDtypeStruct((kv_heads * rows + TERM_ROWS, size), BF16)
    row = jax.ShapeDtypeStruct((1, 128), F32)
    columns = group * rows
    table = jax.ShapeDtypeStruct((8 * (-(-max(reach + 1, kv_heads) // 8)), columns), F32)
    sizes = (kv_heads, group, reach, rows, size)
    span = (reach + 1) * rows

    def along(x, distance):
        return lax.ppermute(x, "ctx", [(i, (i + distance) % count) for i in range(count)])

    def exchanged(x, step, axis="ctx"):
        return lax.ppermute(x, axis, [(i, i ^ step) for i in range(lax.axis_size(axis))])

    keys_before = along(keys, reach)
    own = jnp.concatenate([keys, values], axis=1)
    pair = jnp.concatenate([queries, grad_out], axis=1)
    caps, tops, passed_values = kernel_call(
        functools.partial(tables_kernel, reach, rows, group),
        [table, table, narrow],
        [SMEM] * 3 + [VMEM],
        (place, doc_ids, sinks, own),
    )
    values_before = along(passed_values, reach)

    def gathered(own, chosen, before):
        arrived = [exchanged(chosen[step - 1], step) for step in range(1, reach)]
        return [own, *arrived, before]

    choices = [narrow] * (reach - 1)
    chosen = kernel_call(
        functools.partial(choose_kernel, reach, 0),
        choices,
        [SMEM] + [VMEM] * 3,
        (place, own, keys_before, caps),
    )
    key_blocks = gathered(own, chosen, keys_before)
    chosen = kernel_call(
        functools.partial(choose_kernel, reach, 1), choices, [SMEM] + [VMEM] * 3, (place, own, values_before, pair)
    )
    value_blocks = gathered(own, chosen, values_before)
    probs, sink_probs, values_own, values_share, *messages = kernel_call(
        functools.partial(probs_kernel, *sizes),
        [jax.ShapeDtypeStruct((kv_heads * reach * rows, columns), BF16), table, wide, wide] + [share] * (reach - 1),
        [VMEM] * (4 + reach),
        (caps, tops, pair, *key_blocks),
    )
    values_back = [exchanged(m, step) for step, m in enumerate(messages, 1)]
    gscores, sink_row, keys_own, keys_share, *messages = kernel_call(
        functools.partial(scores_kernel, *sizes),
        [jax.ShapeDtypeStruct((kv_heads * (reach + 1) * rows, columns), BF16), row, wide, wide]
        + [message] * (reach - 1),
        [VMEM] * (4 + reach),
        (probs, sink_probs, pair, *value_blocks),
    )
    keys_back = [exchanged(m, step) for step, m in enumerate(messages, 1)]
    values_own, values_share = kernel_call(
        functools.partial(values_kernel, reach),
        [wide, share],
        [SMEM] + [VMEM] * (reach + 1),
        (place, values_own, values_share, *values_back),
    )
    values_last = along(values_share, -reach)
    keys_own, keys_share, sink_row = kernel_call(
        functools.partial(sums_kernel, reach),
        [wide, message, row],
        [SMEM] + [VMEM] * (reach + 2),
        (place, keys_own, keys_share, sink_row, *keys_back),
    )
    keys_last = along(keys_share, -reach)
    grad_values, grad_queries, done = kernel_call(
        functools.partial(queries_kernel, *sizes),
        [narrow, jax.ShapeDtypeStruct(queries.shape, BF16), row],
        [VMEM] * (4 + reach),
        (gscores, values_own, values_last, *key_blocks),
        2 * rows * group * span * size * kv_heads,
    )
    sink_rows = [sink_row] + [along(sink_row, -distance) for distance in range(2 * reach, count, reach)]
    sink_rows.append(done)
    grad_keys, sink_row = kernel_call(
        totals_kernel,
        [narrow, row],
        [VMEM] * (2 + len(sink_rows)),
        (keys_own, keys_last, *sink_rows),
    )
    if lax.axis_size("dp") == 2:
        sink_row = sink_row + exchanged(sink_row, 1, "dp")
    else:
        sink_row = lax.psum(sink_row, "dp")
    grad_keys, grad_sinks = kernel_call(
        out_kernel, [narrow, jax.ShapeDtypeStruct(sinks.shape, F32)], [VMEM] * 2, (grad_keys, sink_row)
    )
    return grad_queries[None], grad_keys[None], grad_values[None], grad_sinks


def solution(mesh):
    blocks = P("dp", "ctx", None)
    in_specs = (blocks, blocks, blocks, blocks, P(), P("dp", None))
    out_specs = (blocks, blocks, blocks, P())
    return jax.shard_map(local, mesh=mesh, in_specs=in_specs, out_specs=out_specs, check_vma=False)
```

```python
import functools

import jax
import jax.numpy as jnp
from jax import lax
from jax.experimental import pallas as pl
from jax.experimental.pallas import tpu as pltpu
from jax.sharding import PartitionSpec as P

WINDOW = 512
LOG2E = 1.4426950408889634
TERM_ROWS = 16

F32 = jnp.float32
BF16 = jnp.bfloat16
SMEM = pl.BlockSpec(memory_space=pltpu.SMEM)
VMEM = pl.BlockSpec(memory_space=pltpu.VMEM)


def dot_nt(a, b):
    return lax.dot_general(a, b, (((1,), (1,)), ((), ())), preferred_element_type=F32)


def dot_nn(a, b):
    return lax.dot_general(a, b, (((1,), (0,)), ((), ())), preferred_element_type=F32)


def dot_tn(a, b):
    return lax.dot_general(a, b, (((0,), (0,)), ((), ())), preferred_element_type=F32)


def kernel_call(body, out_shape, in_specs, operands, flops=0):
    return pl.pallas_call(
        body,
        out_shape=out_shape,
        in_specs=in_specs,
        out_specs=[VMEM] * len(out_shape),
        compiler_params=pltpu.CompilerParams(vmem_limit_bytes=24 * 1024 * 1024),
        cost_estimate=pl.CostEstimate(flops=flops, bytes_accessed=0, transcendentals=0),
    )(*operands)


def later(slot, step):
    return lax.bitwise_xor(slot, step) > slot


def choose(slot, own, before_ref, out_refs):
    for step, ref in enumerate(out_refs, 1):
        @pl.when(later(slot, step))
        def _():
            ref[...] = own

        @pl.when(jnp.logical_not(later(slot, step)))
        def _():
            ref[...] = before_ref[...]


def choose_kernel(reach, first, place_ref, own_ref, before_ref, *refs):
    width = before_ref.shape[1]
    choose(lax.rem(place_ref[0], reach), own_ref[:, first * width:(first + 1) * width], before_ref, refs[-(reach - 1):])


def tables_kernel(reach, rows, group, place_ref, docs_ref, sinks_ref, own_ref, caps_ref, tops_ref, values_ref):
    values_ref[...] = own_ref[:, values_ref.shape[1]:]
    place = place_ref[0]
    slot = lax.rem(place, reach)
    doc = docs_ref[0, place]
    columns = caps_ref.shape[1]
    for step in range(1, reach + 1):
        distance = reach
        if step < reach:
            distance = lax.rem(slot - lax.bitwise_xor(slot, step) + reach, reach)
        other = docs_ref[0, jnp.maximum(place - distance, 0)]
        same = jnp.logical_and(place >= distance, other == doc)
        caps_ref[step:step + 1, :] = jnp.full((1, columns), jnp.where(same, jnp.inf, -jnp.inf), F32)
    for head in range(sinks_ref.shape[0] // group):
        for j in range(group):
            tops_ref[head:head + 1, j * rows:(j + 1) * rows] = jnp.full(
                (1, rows), sinks_ref[head * group + j] * LOG2E, F32
            )


def block(x, i, rows):
    return x[i * rows:(i + 1) * rows]


def causal_mask(rows, group):
    shape = (rows, group * rows)
    key_at = lax.broadcasted_iota(jnp.int32, shape, 0)
    return key_at <= lax.rem(lax.broadcasted_iota(jnp.int32, shape, 1), rows)


def parted(x, causal):
    zero = jnp.zeros((), x.dtype)
    return jnp.where(causal, x, zero), jnp.where(causal, zero, x)


def split_terms(row):
    parts = []
    for _ in range(3):
        parts.append(row.astype(BF16))
        row = row - parts[-1].astype(F32)
    return jnp.concatenate(parts + [jnp.zeros((TERM_ROWS - 3, row.shape[1]), BF16)], axis=0)


def joined_terms(terms):
    parts = terms.astype(F32)
    return (parts[2:3] + parts[1:2]) + parts[0:1]


def stacked(ref, first, group, size):
    return jnp.concatenate([ref[:, (first + j) * size:(first + j + 1) * size] for j in range(group)], axis=0)


def store_shares(x, head, rows, reach, own_ref, before_ref, message_refs):
    at = slice(head * rows, (head + 1) * rows)
    own_ref[at, :] = block(x, 0, rows)
    before_ref[at, :] = block(x, reach, rows)
    for i, ref in enumerate(message_refs, 1):
        ref[at, :] = block(x, i, rows).astype(BF16)


def softmax_part(s_blocks, caps, top, to_log2):
    sink_log = top
    for i, s in enumerate(s_blocks):
        high = jnp.max(s, axis=0, keepdims=True) * to_log2
        top = jnp.maximum(top, jnp.minimum(high, caps[i]) if i else high)
    sink_weight = jnp.exp2(sink_log - top)
    summed = sink_weight
    raised = []
    for i, s in enumerate(s_blocks):
        e = jnp.exp2(s * to_log2 - (jnp.maximum(top, -caps[i]) if i else top))
        summed = summed + jnp.sum(e, axis=0, keepdims=True)
        raised.append(e)
    inverse = 1.0 / summed
    probs = [(e * inverse).astype(BF16) for e in raised]
    return probs, sink_weight * inverse


def probs_kernel(kv_heads, group, reach, rows, size, caps_ref, tops_ref, pair_ref, *refs):
    blocks = refs[:reach + 1]
    probs_ref, sink_ref, own_ref, before_ref, *message_refs = refs[reach + 1:]
    to_log2 = size ** (-0.5) * LOG2E
    causal = causal_mask(rows, group)
    caps = [caps_ref[i:i + 1, :] for i in range(reach + 1)]

    def scores_of(head):
        cut = slice(head * size, (head + 1) * size)
        q = stacked(pair_ref, head * group, group, size)
        keys = jnp.concatenate([r[:, cut] for r in blocks], axis=0)
        return dot_nt(keys, q)

    waiting = None
    following = scores_of(0)
    for head in range(kv_heads):
        g = stacked(pair_ref, (kv_heads + head) * group, group, size)
        scores = following
        if head + 1 < kv_heads:
            following = scores_of(head + 1)
        s_blocks = [
            jnp.where(causal, block(scores, 0, rows), jnp.minimum(block(scores, reach, rows), caps[reach]))
        ] + [block(scores, i, rows) for i in range(1, reach)]
        parts = []
        for chunk in range(2):
            at = slice(chunk * group * rows // 2, (chunk + 1) * group * rows // 2)
            parts.append(
                softmax_part(
                    [s[:, at] for s in s_blocks], [c[:, at] for c in caps], tops_ref[head:head + 1, at], to_log2
                )
            )
        probs = [jnp.concatenate([p[0][i] for p in parts], axis=1) for i in range(reach)]
        sinkp = jnp.concatenate([p[1] for p in parts], axis=1)
        for i, p in enumerate(probs):
            at = (head * reach + i) * rows
            probs_ref[at:at + rows, :] = p
        sink_ref[head:head + 1, :] = sinkp
        first, last = parted(probs[0], causal)
        if waiting is not None:
            store_shares(dot_nn(*waiting), head - 1, rows, reach, own_ref, before_ref, message_refs)
        waiting = (jnp.concatenate([first] + probs[1:] + [last], axis=0), g)
    store_shares(dot_nn(*waiting), kv_heads - 1, rows, reach, own_ref, before_ref, message_refs)


def scores_kernel(kv_heads, group, reach, rows, size, probs_ref, sinkp_ref, pair_ref, *refs):
    blocks = refs[:reach + 1]
    gscores_ref, sink_ref, own_ref, before_ref, *message_refs = refs[reach + 1:]
    scale = size ** (-0.5)
    columns = group * rows
    causal = causal_mask(rows, group)
    lane = lax.broadcasted_iota(jnp.int32, (1, 128), 1)
    sink_row = jnp.zeros((1, 128), F32)

    def gprobs_of(head):
        cut = slice(head * size, (head + 1) * size)
        g = stacked(pair_ref, (kv_heads + head) * group, group, size)
        own_cut = slice((kv_heads + head) * size, (kv_heads + head + 1) * size)
        values = jnp.concatenate([blocks[0][:, own_cut]] + [r[:, cut] for r in blocks[1:]], axis=0)
        return dot_nt(values, g)

    waiting = None
    following = gprobs_of(0)
    for head in range(kv_heads):
        q = stacked(pair_ref, head * group, group, size)
        gprobs = following
        if head + 1 < kv_heads:
            following = gprobs_of(head + 1)
        t_blocks = [jnp.where(causal, block(gprobs, 0, rows), block(gprobs, reach, rows))]
        t_blocks += [block(gprobs, i, rows) for i in range(1, reach)]
        probs = [
            probs_ref[(head * reach + i) * rows:(head * reach + i + 1) * rows, :].astype(F32) for i in range(reach)
        ]
        delta = jnp.zeros((1, columns), F32)
        for p, t in zip(probs, t_blocks):
            delta = delta + jnp.sum(p * t, axis=0, keepdims=True)
        gscores = [(p * (t - delta)).astype(BF16) for p, t in zip(probs, t_blocks)]
        first, last = parted(gscores[0], causal)
        gscores = jnp.concatenate([first] + gscores[1:] + [last], axis=0)
        span = (reach + 1) * rows
        gscores_ref[head * span:(head + 1) * span, :] = gscores
        if waiting is not None:
            store_shares(dot_nn(*waiting) * scale, head - 1, rows, reach, own_ref, before_ref, message_refs)
        waiting = (gscores, q)
        sink_terms = sinkp_ref[head:head + 1, :] * delta
        for j in range(group):
            term = jnp.sum(sink_terms[:, j * rows:(j + 1) * rows], axis=1, keepdims=True)
            sink_row = jnp.where(lane == head * group + j, -term, sink_row)
    store_shares(dot_nn(*waiting) * scale, kv_heads - 1, rows, reach, own_ref, before_ref, message_refs)
    sink_ref[...] = sink_row
    terms = split_terms(sink_row)
    for ref in message_refs:
        ref[kv_heads * rows:, :] = terms


def queries_kernel(kv_heads, group, reach, rows, size, gscores_ref, own_ref, last_ref, *refs):
    *blocks, dv_ref, dq_ref, done_ref = refs
    side_by_side(own_ref, last_ref[...], dv_ref)
    scale = size ** (-0.5)
    span = (reach + 1) * rows
    for head in range(kv_heads):
        cut = slice(head * size, (head + 1) * size)
        keys = jnp.concatenate([r[:, cut] for r in blocks], axis=0)
        dq = (dot_tn(gscores_ref[head * span:(head + 1) * span, :], keys) * scale).astype(BF16)
        for j in range(group):
            at = (head * group + j) * size
            dq_ref[:, at:at + size] = dq[j * rows:(j + 1) * rows]
    done_ref[...] = jnp.zeros_like(done_ref)


def combine(reach, place_ref, own_ref, before_ref, messages, own_out, before_out):
    slot = lax.rem(place_ref[0], reach)
    own, before = own_ref[...], before_ref[...]
    for step, message in enumerate(messages, 1):
        mine = later(slot, step)
        back = message[:own.shape[0], :].astype(F32)
        own = own + jnp.where(mine, back, 0.0)
        before = before + jnp.where(mine, 0.0, back)
    own_out[...] = own
    before_out[...] = before.astype(BF16)


def values_kernel(reach, place_ref, own_ref, before_ref, *refs):
    *messages, own_out, before_out = refs
    combine(reach, place_ref, own_ref, before_ref, messages, own_out, before_out)


def sums_kernel(reach, place_ref, own_ref, before_ref, sink_ref, *refs):
    *messages, own_out, before_out, sink_out = refs
    height = own_ref.shape[0]
    combine(reach, place_ref, own_ref, before_ref, messages, own_out, before_out.at[:height, :])
    sink_row = sink_ref[...]
    for message in messages:
        sink_row = sink_row + joined_terms(message[height:, :])
    before_out[height:, :] = split_terms(sink_row)
    sink_out[...] = sink_row


def side_by_side(own_ref, last, out_ref):
    rows, width = out_ref.shape
    total = own_ref[...] + last.astype(F32)
    size = total.shape[1]
    for head in range(width // size):
        out_ref[:, head * size:(head + 1) * size] = block(total, head, rows).astype(BF16)


def planes_kernel(last_ref, sink_ref, *refs):
    *sink_refs, sink_out = refs
    sink_row = sink_ref[...] + joined_terms(last_ref[last_ref.shape[0] - TERM_ROWS:, :])
    for ref in sink_refs:
        sink_row = sink_row + ref[...]
    sink_out[...] = sink_row


def keys_end_kernel(own_ref, last_ref, keys_out, done_ref):
    side_by_side(own_ref, last_ref[:own_ref.shape[0], :], keys_out)
    done_ref[...] = jnp.zeros_like(done_ref)


def out_kernel(sink_ref, done_ref, sink_out):
    sink_out[...] = (sink_ref[...] + done_ref[...])[0, :sink_out.shape[0]]


def local(queries, keys, values, grad_out, sinks, doc_ids):
    rows, q_width = queries.shape[1:]
    kv_width = keys.shape[2]
    heads = sinks.shape[0]
    size = q_width // heads
    group = q_width // kv_width
    kv_heads = kv_width // size
    reach = WINDOW // rows
    count = lax.axis_size("ctx")
    place = jnp.full((1,), lax.axis_index("ctx"), jnp.int32)
    queries, keys, values, grad_out = queries[0], keys[0], values[0], grad_out[0]
    narrow = jax.ShapeDtypeStruct(keys.shape, BF16)
    wide = jax.ShapeDtypeStruct((kv_heads * rows, size), F32)
    share = jax.ShapeDtypeStruct(wide.shape, BF16)
    message = jax.ShapeDtypeStruct((kv_heads * rows + TERM_ROWS, size), BF16)
    row = jax.ShapeDtypeStruct((1, 128), F32)
    columns = group * rows
    table = jax.ShapeDtypeStruct((8 * (-(-max(reach + 1, kv_heads) // 8)), columns), F32)
    sizes = (kv_heads, group, reach, rows, size)
    span = (reach + 1) * rows

    def along(x, distance):
        return lax.ppermute(x, "ctx", [(i, (i + distance) % count) for i in range(count)])

    def exchanged(x, step, axis="ctx"):
        return lax.ppermute(x, axis, [(i, i ^ step) for i in range(lax.axis_size(axis))])

    keys_before = along(keys, reach)
    own = jnp.concatenate([keys, values], axis=1)
    pair = jnp.concatenate([queries, grad_out], axis=1)
    caps, tops, passed_values = kernel_call(
        functools.partial(tables_kernel, reach, rows, group),
        [table, table, narrow],
        [SMEM] * 3 + [VMEM],
        (place, doc_ids, sinks, own),
    )
    values_before = along(passed_values, reach)

    def gathered(own, chosen, before):
        arrived = [exchanged(chosen[step - 1], step) for step in range(1, reach)]
        return [own, *arrived, before]

    choices = [narrow] * (reach - 1)
    chosen = kernel_call(
        functools.partial(choose_kernel, reach, 0),
        choices,
        [SMEM] + [VMEM] * 3,
        (place, own, keys_before, caps),
    )
    key_blocks = gathered(own, chosen, keys_before)
    chosen = kernel_call(
        functools.partial(choose_kernel, reach, 1), choices, [SMEM] + [VMEM] * 3, (place, own, values_before, pair)
    )
    value_blocks = gathered(own, chosen, values_before)
    probs, sink_probs, values_own, values_share, *messages = kernel_call(
        functools.partial(probs_kernel, *sizes),
        [jax.ShapeDtypeStruct((kv_heads * reach * rows, columns), BF16), table, wide, wide] + [share] * (reach - 1),
        [VMEM] * (4 + reach),
        (caps, tops, pair, *key_blocks),
    )
    values_back = [exchanged(m, step) for step, m in enumerate(messages, 1)]
    gscores, sink_row, keys_own, keys_share, *messages = kernel_call(
        functools.partial(scores_kernel, *sizes),
        [jax.ShapeDtypeStruct((kv_heads * (reach + 1) * rows, columns), BF16), row, wide, wide]
        + [message] * (reach - 1),
        [VMEM] * (4 + reach),
        (probs, sink_probs, pair, *value_blocks),
    )
    keys_back = [exchanged(m, step) for step, m in enumerate(messages, 1)]
    values_own, values_share = kernel_call(
        functools.partial(values_kernel, reach),
        [wide, share],
        [SMEM] + [VMEM] * (reach + 1),
        (place, values_own, values_share, *values_back),
    )
    values_last = along(values_share, -reach)
    keys_own, keys_share, sink_row = kernel_call(
        functools.partial(sums_kernel, reach),
        [wide, message, row],
        [SMEM] + [VMEM] * (reach + 2),
        (place, keys_own, keys_share, sink_row, *keys_back),
    )
    keys_last = along(keys_share, -reach)
    grad_values, grad_queries, done = kernel_call(
        functools.partial(queries_kernel, *sizes),
        [narrow, jax.ShapeDtypeStruct(queries.shape, BF16), row],
        [VMEM] * (4 + reach),
        (gscores, values_own, values_last, *key_blocks),
        2 * rows * group * span * size * kv_heads,
    )
    sink_rows = [sink_row] + [along(sink_row, -distance) for distance in range(2 * reach, count, reach)]
    sink_rows.append(done)
    sink_row, = kernel_call(planes_kernel, [row], [VMEM] * (1 + len(sink_rows)), (keys_last, *sink_rows))
    grad_keys, done = kernel_call(keys_end_kernel, [narrow, row], [VMEM] * 2, (keys_own, keys_last))
    if lax.axis_size("dp") == 2:
        sink_row = sink_row + exchanged(sink_row, 1, "dp")
    else:
        sink_row = lax.psum(sink_row, "dp")
    grad_sinks, = kernel_call(out_kernel, [jax.ShapeDtypeStruct(sinks.shape, F32)], [VMEM] * 2, (sink_row, done))
    return grad_queries[None], grad_keys[None], grad_values[None], grad_sinks


def solution(mesh):
    blocks = P("dp", "ctx", None)
    in_specs = (blocks, blocks, blocks, blocks, P(), P("dp", None))
    out_specs = (blocks, blocks, blocks, P())
    return jax.shard_map(local, mesh=mesh, in_specs=in_specs, out_specs=out_specs, check_vma=False)
```

```python
import functools

import jax
import jax.numpy as jnp
from jax import lax
from jax.experimental import pallas as pl
from jax.experimental.pallas import tpu as pltpu
from jax.sharding import PartitionSpec as P

WINDOW = 512
LOG2E = 1.4426950408889634
TERM_ROWS = 16

F32 = jnp.float32
BF16 = jnp.bfloat16
SMEM = pl.BlockSpec(memory_space=pltpu.SMEM)
VMEM = pl.BlockSpec(memory_space=pltpu.VMEM)


def dot_nt(a, b):
    return lax.dot_general(a, b, (((1,), (1,)), ((), ())), preferred_element_type=F32)


def dot_nn(a, b):
    return lax.dot_general(a, b, (((1,), (0,)), ((), ())), preferred_element_type=F32)


def dot_tn(a, b):
    return lax.dot_general(a, b, (((0,), (0,)), ((), ())), preferred_element_type=F32)


def kernel_call(body, out_shape, in_specs, operands, flops=0):
    return pl.pallas_call(
        body,
        out_shape=out_shape,
        in_specs=in_specs,
        out_specs=[VMEM] * len(out_shape),
        compiler_params=pltpu.CompilerParams(vmem_limit_bytes=24 * 1024 * 1024),
        cost_estimate=pl.CostEstimate(flops=flops, bytes_accessed=0, transcendentals=0),
    )(*operands)


def later(slot, step):
    return lax.bitwise_xor(slot, step) > slot


def choose(slot, own, before_ref, out_refs):
    for step, ref in enumerate(out_refs, 1):
        @pl.when(later(slot, step))
        def _():
            ref[...] = own

        @pl.when(jnp.logical_not(later(slot, step)))
        def _():
            ref[...] = before_ref[...]


def choose_kernel(reach, first, place_ref, own_ref, before_ref, *refs):
    width = before_ref.shape[1]
    choose(lax.rem(place_ref[0], reach), own_ref[:, first * width:(first + 1) * width], before_ref, refs[-(reach - 1):])


def tables_kernel(reach, rows, group, place_ref, docs_ref, sinks_ref, own_ref, caps_ref, tops_ref, values_ref):
    values_ref[...] = own_ref[:, values_ref.shape[1]:]
    place = place_ref[0]
    slot = lax.rem(place, reach)
    doc = docs_ref[0, place]
    columns = caps_ref.shape[1]
    for step in range(1, reach + 1):
        distance = reach
        if step < reach:
            distance = lax.rem(slot - lax.bitwise_xor(slot, step) + reach, reach)
        other = docs_ref[0, jnp.maximum(place - distance, 0)]
        same = jnp.logical_and(place >= distance, other == doc)
        caps_ref[step:step + 1, :] = jnp.full((1, columns), jnp.where(same, jnp.inf, -jnp.inf), F32)
    for head in range(sinks_ref.shape[0] // group):
        for j in range(group):
            tops_ref[head:head + 1, j * rows:(j + 1) * rows] = jnp.full(
                (1, rows), sinks_ref[head * group + j] * LOG2E, F32
            )


def block(x, i, rows):
    return x[i * rows:(i + 1) * rows]


def causal_mask(rows, group):
    shape = (rows, group * rows)
    key_at = lax.broadcasted_iota(jnp.int32, shape, 0)
    return key_at <= lax.rem(lax.broadcasted_iota(jnp.int32, shape, 1), rows)


def parted(x, causal):
    zero = jnp.zeros((), x.dtype)
    return jnp.where(causal, x, zero), jnp.where(causal, zero, x)


def split_terms(row):
    parts = []
    for _ in range(3):
        parts.append(row.astype(BF16))
        row = row - parts[-1].astype(F32)
    return jnp.concatenate(parts + [jnp.zeros((TERM_ROWS - 3, row.shape[1]), BF16)], axis=0)


def joined_terms(terms):
    parts = terms.astype(F32)
    return (parts[2:3] + parts[1:2]) + parts[0:1]


def stacked(ref, first, group, size):
    return jnp.concatenate([ref[:, (first + j) * size:(first + j + 1) * size] for j in range(group)], axis=0)


def store_shares(x, head, rows, reach, own_ref, before_ref, message_refs):
    at = slice(head * rows, (head + 1) * rows)
    own_ref[at, :] = block(x, 0, rows)
    before_ref[at, :] = block(x, reach, rows)
    for i, ref in enumerate(message_refs, 1):
        ref[at, :] = block(x, i, rows).astype(BF16)


def softmax_part(s_blocks, caps, top, to_log2):
    sink_log = top
    for i, s in enumerate(s_blocks):
        high = jnp.max(s, axis=0, keepdims=True) * to_log2
        top = jnp.maximum(top, jnp.minimum(high, caps[i]) if i else high)
    sink_weight = jnp.exp2(sink_log - top)
    summed = sink_weight
    raised = []
    for i, s in enumerate(s_blocks):
        e = jnp.exp2(s * to_log2 - (jnp.maximum(top, -caps[i]) if i else top))
        summed = summed + jnp.sum(e, axis=0, keepdims=True)
        raised.append(e)
    inverse = 1.0 / summed
    probs = [(e * inverse).astype(BF16) for e in raised]
    return probs, sink_weight * inverse


def probs_kernel(kv_heads, group, reach, rows, size, caps_ref, tops_ref, pair_ref, *refs):
    blocks = refs[:reach + 1]
    probs_ref, sink_ref, own_ref, before_ref, *message_refs = refs[reach + 1:]
    to_log2 = size ** (-0.5) * LOG2E
    causal = causal_mask(rows, group)
    caps = [caps_ref[i:i + 1, :] for i in range(reach + 1)]

    def scores_of(head):
        cut = slice(head * size, (head + 1) * size)
        q = stacked(pair_ref, head * group, group, size)
        keys = jnp.concatenate([r[:, cut] for r in blocks], axis=0)
        return dot_nt(keys, q)

    waiting = None
    following = scores_of(0)
    for head in range(kv_heads):
        g = stacked(pair_ref, (kv_heads + head) * group, group, size)
        scores = following
        if head + 1 < kv_heads:
            following = scores_of(head + 1)
        s_blocks = [
            jnp.where(causal, block(scores, 0, rows), jnp.minimum(block(scores, reach, rows), caps[reach]))
        ] + [block(scores, i, rows) for i in range(1, reach)]
        parts = []
        for chunk in range(2):
            at = slice(chunk * group * rows // 2, (chunk + 1) * group * rows // 2)
            parts.append(
                softmax_part(
                    [s[:, at] for s in s_blocks], [c[:, at] for c in caps], tops_ref[head:head + 1, at], to_log2
                )
            )
        probs = [jnp.concatenate([p[0][i] for p in parts], axis=1) for i in range(reach)]
        sinkp = jnp.concatenate([p[1] for p in parts], axis=1)
        for i, p in enumerate(probs):
            at = (head * reach + i) * rows
            probs_ref[at:at + rows, :] = p
        sink_ref[head:head + 1, :] = sinkp
        first, last = parted(probs[0], causal)
        if waiting is not None:
            store_shares(dot_nn(*waiting), head - 1, rows, reach, own_ref, before_ref, message_refs)
        waiting = (jnp.concatenate([first] + probs[1:] + [last], axis=0), g)
    store_shares(dot_nn(*waiting), kv_heads - 1, rows, reach, own_ref, before_ref, message_refs)


def scores_kernel(kv_heads, group, reach, rows, size, probs_ref, sinkp_ref, pair_ref, *refs):
    blocks = refs[:reach + 1]
    gscores_ref, sink_ref, own_ref, before_ref, *message_refs = refs[reach + 1:]
    scale = size ** (-0.5)
    columns = group * rows
    causal = causal_mask(rows, group)
    lane = lax.broadcasted_iota(jnp.int32, (1, 128), 1)
    sink_row = jnp.zeros((1, 128), F32)

    def gprobs_of(head):
        cut = slice(head * size, (head + 1) * size)
        g = stacked(pair_ref, (kv_heads + head) * group, group, size)
        own_cut = slice((kv_heads + head) * size, (kv_heads + head + 1) * size)
        values = jnp.concatenate([blocks[0][:, own_cut]] + [r[:, cut] for r in blocks[1:]], axis=0)
        return dot_nt(values, g)

    waiting = None
    following = gprobs_of(0)
    for head in range(kv_heads):
        q = stacked(pair_ref, head * group, group, size)
        gprobs = following
        if head + 1 < kv_heads:
            following = gprobs_of(head + 1)
        t_blocks = [jnp.where(causal, block(gprobs, 0, rows), block(gprobs, reach, rows))]
        t_blocks += [block(gprobs, i, rows) for i in range(1, reach)]
        probs = [
            probs_ref[(head * reach + i) * rows:(head * reach + i + 1) * rows, :].astype(F32) for i in range(reach)
        ]
        delta = jnp.zeros((1, columns), F32)
        for p, t in zip(probs, t_blocks):
            delta = delta + jnp.sum(p * t, axis=0, keepdims=True)
        gscores = [(p * (t - delta)).astype(BF16) for p, t in zip(probs, t_blocks)]
        first, last = parted(gscores[0], causal)
        gscores = jnp.concatenate([first] + gscores[1:] + [last], axis=0)
        span = (reach + 1) * rows
        gscores_ref[head * span:(head + 1) * span, :] = gscores
        if waiting is not None:
            store_shares(dot_nn(*waiting) * scale, head - 1, rows, reach, own_ref, before_ref, message_refs)
        waiting = (gscores, q)
        sink_terms = sinkp_ref[head:head + 1, :] * delta
        for j in range(group):
            term = jnp.sum(sink_terms[:, j * rows:(j + 1) * rows], axis=1, keepdims=True)
            sink_row = jnp.where(lane == head * group + j, -term, sink_row)
    store_shares(dot_nn(*waiting) * scale, kv_heads - 1, rows, reach, own_ref, before_ref, message_refs)
    sink_ref[...] = sink_row
    terms = split_terms(sink_row)
    for ref in message_refs:
        ref[kv_heads * rows:, :] = terms


def queries_kernel(kv_heads, group, reach, rows, size, gscores_ref, own_ref, last_ref, *refs):
    *blocks, dv_ref, dq_ref, done_ref = refs
    side_by_side(own_ref, last_ref[...], dv_ref)
    scale = size ** (-0.5)
    span = (reach + 1) * rows
    for head in range(kv_heads):
        cut = slice(head * size, (head + 1) * size)
        keys = jnp.concatenate([r[:, cut] for r in blocks], axis=0)
        dq = jnp.transpose((dot_tn(keys, gscores_ref[head * span:(head + 1) * span, :]) * scale).astype(BF16))
        for j in range(group):
            at = (head * group + j) * size
            dq_ref[:, at:at + size] = dq[j * rows:(j + 1) * rows]
    done_ref[...] = jnp.zeros_like(done_ref)


def combine(reach, place_ref, own_ref, before_ref, messages, own_out, before_out):
    slot = lax.rem(place_ref[0], reach)
    own, before = own_ref[...], before_ref[...]
    for step, message in enumerate(messages, 1):
        mine = later(slot, step)
        back = message[:own.shape[0], :].astype(F32)
        own = own + jnp.where(mine, back, 0.0)
        before = before + jnp.where(mine, 0.0, back)
    own_out[...] = own
    before_out[...] = before.astype(BF16)


def values_kernel(reach, place_ref, own_ref, before_ref, *refs):
    *messages, own_out, before_out = refs
    combine(reach, place_ref, own_ref, before_ref, messages, own_out, before_out)


def sums_kernel(reach, place_ref, own_ref, before_ref, sink_ref, *refs):
    *messages, own_out, before_out, sink_out = refs
    height = own_ref.shape[0]
    combine(reach, place_ref, own_ref, before_ref, messages, own_out, before_out.at[:height, :])
    sink_row = sink_ref[...]
    for message in messages:
        sink_row = sink_row + joined_terms(message[height:, :])
    before_out[height:, :] = split_terms(sink_row)
    sink_out[...] = sink_row


def side_by_side(own_ref, last, out_ref):
    rows, width = out_ref.shape
    total = own_ref[...] + last.astype(F32)
    size = total.shape[1]
    for head in range(width // size):
        out_ref[:, head * size:(head + 1) * size] = block(total, head, rows).astype(BF16)


def planes_kernel(last_ref, sink_ref, *refs):
    *sink_refs, sink_out = refs
    sink_row = sink_ref[...] + joined_terms(last_ref[last_ref.shape[0] - TERM_ROWS:, :])
    for ref in sink_refs:
        sink_row = sink_row + ref[...]
    sink_out[...] = sink_row


def keys_end_kernel(own_ref, last_ref, keys_out, done_ref):
    side_by_side(own_ref, last_ref[:own_ref.shape[0], :], keys_out)
    done_ref[...] = jnp.zeros_like(done_ref)


def out_kernel(sink_ref, done_ref, sink_out):
    sink_out[...] = (sink_ref[...] + done_ref[...])[0, :sink_out.shape[0]]


def local(queries, keys, values, grad_out, sinks, doc_ids):
    rows, q_width = queries.shape[1:]
    kv_width = keys.shape[2]
    heads = sinks.shape[0]
    size = q_width // heads
    group = q_width // kv_width
    kv_heads = kv_width // size
    reach = WINDOW // rows
    count = lax.axis_size("ctx")
    place = jnp.full((1,), lax.axis_index("ctx"), jnp.int32)
    queries, keys, values, grad_out = queries[0], keys[0], values[0], grad_out[0]
    narrow = jax.ShapeDtypeStruct(keys.shape, BF16)
    wide = jax.ShapeDtypeStruct((kv_heads * rows, size), F32)
    share = jax.ShapeDtypeStruct(wide.shape, BF16)
    message = jax.ShapeDtypeStruct((kv_heads * rows + TERM_ROWS, size), BF16)
    row = jax.ShapeDtypeStruct((1, 128), F32)
    columns = group * rows
    table = jax.ShapeDtypeStruct((8 * (-(-max(reach + 1, kv_heads) // 8)), columns), F32)
    sizes = (kv_heads, group, reach, rows, size)
    span = (reach + 1) * rows

    def along(x, distance):
        return lax.ppermute(x, "ctx", [(i, (i + distance) % count) for i in range(count)])

    def exchanged(x, step, axis="ctx"):
        return lax.ppermute(x, axis, [(i, i ^ step) for i in range(lax.axis_size(axis))])

    keys_before = along(keys, reach)
    own = jnp.concatenate([keys, values], axis=1)
    pair = jnp.concatenate([queries, grad_out], axis=1)
    caps, tops, passed_values = kernel_call(
        functools.partial(tables_kernel, reach, rows, group),
        [table, table, narrow],
        [SMEM] * 3 + [VMEM],
        (place, doc_ids, sinks, own),
    )
    values_before = along(passed_values, reach)

    def gathered(own, chosen, before):
        arrived = [exchanged(chosen[step - 1], step) for step in range(1, reach)]
        return [own, *arrived, before]

    choices = [narrow] * (reach - 1)
    chosen = kernel_call(
        functools.partial(choose_kernel, reach, 0),
        choices,
        [SMEM] + [VMEM] * 3,
        (place, own, keys_before, caps),
    )
    key_blocks = gathered(own, chosen, keys_before)
    chosen = kernel_call(
        functools.partial(choose_kernel, reach, 1), choices, [SMEM] + [VMEM] * 3, (place, own, values_before, pair)
    )
    value_blocks = gathered(own, chosen, values_before)
    probs, sink_probs, values_own, values_share, *messages = kernel_call(
        functools.partial(probs_kernel, *sizes),
        [jax.ShapeDtypeStruct((kv_heads * reach * rows, columns), BF16), table, wide, wide] + [share] * (reach - 1),
        [VMEM] * (4 + reach),
        (caps, tops, pair, *key_blocks),
    )
    values_back = [exchanged(m, step) for step, m in enumerate(messages, 1)]
    gscores, sink_row, keys_own, keys_share, *messages = kernel_call(
        functools.partial(scores_kernel, *sizes),
        [jax.ShapeDtypeStruct((kv_heads * (reach + 1) * rows, columns), BF16), row, wide, wide]
        + [message] * (reach - 1),
        [VMEM] * (4 + reach),
        (probs, sink_probs, pair, *value_blocks),
    )
    keys_back = [exchanged(m, step) for step, m in enumerate(messages, 1)]
    values_own, values_share = kernel_call(
        functools.partial(values_kernel, reach),
        [wide, share],
        [SMEM] + [VMEM] * (reach + 1),
        (place, values_own, values_share, *values_back),
    )
    values_last = along(values_share, -reach)
    keys_own, keys_share, sink_row = kernel_call(
        functools.partial(sums_kernel, reach),
        [wide, message, row],
        [SMEM] + [VMEM] * (reach + 2),
        (place, keys_own, keys_share, sink_row, *keys_back),
    )
    keys_last = along(keys_share, -reach)
    grad_values, grad_queries, done = kernel_call(
        functools.partial(queries_kernel, *sizes),
        [narrow, jax.ShapeDtypeStruct(queries.shape, BF16), row],
        [VMEM] * (4 + reach),
        (gscores, values_own, values_last, *key_blocks),
        2 * rows * group * span * size * kv_heads,
    )
    sink_rows = [sink_row] + [along(sink_row, -distance) for distance in range(2 * reach, count, reach)]
    sink_rows.append(done)
    sink_row, = kernel_call(planes_kernel, [row], [VMEM] * (1 + len(sink_rows)), (keys_last, *sink_rows))
    grad_keys, done = kernel_call(keys_end_kernel, [narrow, row], [VMEM] * 2, (keys_own, keys_last))
    if lax.axis_size("dp") == 2:
        sink_row = sink_row + exchanged(sink_row, 1, "dp")
    else:
        sink_row = lax.psum(sink_row, "dp")
    grad_sinks, = kernel_call(out_kernel, [jax.ShapeDtypeStruct(sinks.shape, F32)], [VMEM] * 2, (sink_row, done))
    return grad_queries[None], grad_keys[None], grad_values[None], grad_sinks


def solution(mesh):
    blocks = P("dp", "ctx", None)
    in_specs = (blocks, blocks, blocks, blocks, P(), P("dp", None))
    out_specs = (blocks, blocks, blocks, P())
    return jax.shard_map(local, mesh=mesh, in_specs=in_specs, out_specs=out_specs, check_vma=False)
```
